512 devices in a mesh: dp: 16 (over x, z_hi, core), seq: 32 (over z_lo, y).
Axes of the slice: x: 4, y: 8, z: 8 (z_hi: 2, z_lo: 4; z = z_hi * 4 + z_lo), core: 2. Of those that a mesh axis runs over, the one named last changes fastest.
Arguments:
- tokens: bfloat16 [16, 32, 128, 1152], P('dp', 'seq'), may hold values from -6 to 6
- modulation: float32 [16, 6, 1152], P('dp'), may hold values from -0.8 to 0.8
- spatial_project: bfloat16 [1152, 1728], P('seq'), may hold values from -4 to 4
- spatial_merge: bfloat16 [576, 1152], P('seq'), may hold values from -0.25 to 0.25
- temporal_project: bfloat16 [1152, 1728], P('seq'), may hold values from -4 to 4
- temporal_merge: bfloat16 [576, 1152], P('seq'), may hold values from -0.25 to 0.25
- cotangent: bfloat16 [16, 16, 2, 128, 1152], P('dp', None, None, 'seq'), may hold values from -6 to 6
Outputs:
- result: bfloat16 [16, 16, 2, 128, 1152], P('dp', None, None, 'seq')
- token_grads: bfloat16 [16, 32, 128, 1152], P('dp', 'seq')
- merge_grads: float32 [576, 1152], P('seq')
The draws below stay inside these ranges and needn't reach their ends.
All inputs are finite; a program needn't handle non-finite values.
Results may differ from the reference program's by a relative error of at most 0.035.
Values may be sent and summed in bfloat16 or wider, within the bound.
A program may use at most 64 MiB of HBM per device.

```python
import jax
import jax.numpy as jnp
from jax import lax

D = 1152
HEAD_DIM = 72
HEADS = 8
HW = 576
FRAMES = 16
PATCHES = 256
HALF = 128
CLIPS = 16


def projection_draw(key):
    first_key = jax.random.fold_in(key, 0)
    inner_width = HEADS * HEAD_DIM
    entries = jax.random.truncated_normal(first_key, -4.0, 4.0, (D, 3 * inner_width), jnp.float32) * D ** (-0.5)
    query_part = entries[:, :inner_width]
    key_part = entries[:, inner_width:2 * inner_width]
    key_part = jnp.clip(key_part, -4.0, 4.0)
    return jnp.concatenate([query_part, key_part, entries[:, 2 * inner_width:]], 1).astype(jnp.bfloat16)


def draw_spatial_project(key, part):
    key = jax.random.fold_in(key, 5)
    return projection_draw(key)


def draw_temporal_project(key, part):
    key = jax.random.fold_in(key, 9)
    return projection_draw(key)


def steps_of(key, shape, shards, low, high):
    factor_of = 1.0
    for axis_at, blocks in shards:
        steps = jax.random.uniform(jax.random.fold_in(jax.random.fold_in(key, 6), axis_at), (blocks,), jnp.float32, low / len(shards), high / len(shards))
        factor_of = factor_of * jnp.repeat(jnp.exp(steps), shape[axis_at] // blocks).reshape((-1,) + (1,) * (len(shape) - 1 - axis_at))
    return factor_of


def noise(stream_key, dims, width, most, cuts=(), kind=jnp.bfloat16):
    values = width * jax.random.normal(stream_key, dims, jnp.float32)
    if cuts:
        values = values * steps_of(stream_key, dims, cuts, -0.22, 0.18)
    return jnp.clip(values, -most, most).astype(kind)


def setup_inputs(seed: int = 0) -> dict:
    arg_keys = jax.random.split(jax.random.key(seed), 8)
    return {
        "tokens": noise(arg_keys[0], (CLIPS, 2 * FRAMES, HALF, D), 1.0, 6.0, ((0, 16), (1, 32))),
        "modulation": jnp.clip(jax.random.uniform(arg_keys[1], (CLIPS, 6, D), jnp.float32, -0.8, 0.8) * steps_of(arg_keys[1], (CLIPS, 6, D), ((0, 16),), -0.4, 0.0), -0.8, 0.8),
        "spatial_project": draw_spatial_project(jax.random.fold_in(arg_keys[7], 71), 0),
        "spatial_merge": noise(arg_keys[3], (HW, D), HW ** -0.5, 0.25, ((0, 32),)),
        "temporal_project": draw_temporal_project(jax.random.fold_in(arg_keys[7], 71), 0),
        "temporal_merge": noise(arg_keys[5], (HW, D), HW ** -0.5, 0.25, ((0, 32),)),
        "cotangent": noise(arg_keys[6], (CLIPS, FRAMES, 2, HALF, D), 1.0, 6.0, ((0, 16), (3, 32))),
    }


EPSILON = 1e-06
FORMS = ('bqhe,bkhe->bhqk', 'bhqk,bkhe->bqhe', 'bhqk,bqhe->bkhe')

def modulate(tokens_in, shift_row, scale_row):
    widened = tokens_in.astype(jnp.float32)
    average = lax.optimization_barrier(jnp.mean(widened, -1, keepdims=True))
    centered = widened - average
    variance = lax.optimization_barrier(jnp.mean(centered * centered, -1, keepdims=True))
    inverse_std = lax.rsqrt(variance + EPSILON)
    normed = centered * inverse_std
    modulated = (normed * (1.0 + scale_row) + shift_row).astype(jnp.bfloat16)
    return (modulated, normed, inverse_std)

def modulate_back(grad_modulated, normed, inverse_std, scale_row):
    grad_normed = grad_modulated * (1.0 + scale_row)
    first_mean = lax.optimization_barrier(jnp.mean(grad_normed, -1, keepdims=True))
    second_mean = lax.optimization_barrier(jnp.mean(grad_normed * normed, -1, keepdims=True))
    return inverse_std * (grad_normed - first_mean - normed * second_mean)

def attend(queries, keys_all, values_all):
    factor = HEAD_DIM ** (-0.5)
    scores = jnp.einsum(FORMS[0], queries.astype(jnp.float32), keys_all.astype(jnp.float32)) * factor
    probs = jax.nn.softmax(scores, -1)
    weights16 = probs.astype(jnp.bfloat16)
    attended = jnp.einsum(FORMS[1], weights16.astype(jnp.float32), values_all.astype(jnp.float32))
    return (attended.astype(jnp.bfloat16), probs)

def attend_back(queries, keys_all, values_all, probs, grad_attended):
    factor = HEAD_DIM ** (-0.5)
    weights16 = probs.astype(jnp.bfloat16).astype(jnp.float32)
    grad_wide = grad_attended.astype(jnp.float32)
    grad_probs = jnp.einsum(FORMS[0], grad_wide, values_all.astype(jnp.float32))
    grad_values = jnp.einsum(FORMS[2], weights16, grad_wide)
    totals = lax.optimization_barrier(jnp.sum(probs * grad_probs, -1, keepdims=True))
    grad_scores = (probs * (grad_probs - totals) * factor).astype(jnp.bfloat16).astype(jnp.float32)
    grad_queries = jnp.einsum(FORMS[1], grad_scores, keys_all.astype(jnp.float32))
    grad_keys = jnp.einsum(FORMS[2], grad_scores, queries.astype(jnp.float32))
    return (grad_queries, grad_keys, grad_values)

def block_forward(tokens_in, project, merge, shift_row, scale_row, gate_row):
    batch_count, length, model_width = tokens_in.shape
    inner_width = merge.shape[0]
    head_count = inner_width // HEAD_DIM
    modulated, normed, inverse_std = modulate(tokens_in, shift_row, scale_row)
    packed = jnp.dot(modulated.reshape(batch_count * length, model_width), project, preferred_element_type=jnp.float32)
    packed = packed.astype(jnp.bfloat16).reshape(batch_count, length, 3, head_count, HEAD_DIM)
    queries, keys_all, values_all = (packed[:, :, 0], packed[:, :, 1], packed[:, :, 2])
    attended, probs = attend(queries, keys_all, values_all)
    flat_rows = attended.reshape(batch_count * length, inner_width)
    branch = jnp.dot(flat_rows, merge, preferred_element_type=jnp.float32).reshape(batch_count, length, model_width)
    output = (tokens_in.astype(jnp.float32) + gate_row * branch).astype(jnp.bfloat16)
    return (output, (normed, inverse_std, queries, keys_all, values_all, probs, flat_rows))

def block_backward(grad_out, project, merge, scale_row, gate_row, saved):
    normed, inverse_std, queries, keys_all, values_all, probs, flat_rows = saved
    batch_count, length, model_width = grad_out.shape
    inner_width = merge.shape[0]
    head_count = inner_width // HEAD_DIM
    scaled = (gate_row * grad_out.astype(jnp.float32)).astype(jnp.bfloat16).reshape(batch_count * length, model_width)
    grad_attended = lax.dot_general(scaled, merge, (((1,), (1,)), ((), ())), preferred_element_type=jnp.float32)
    grad_attended = grad_attended.astype(jnp.bfloat16).reshape(batch_count, length, head_count, HEAD_DIM)
    merge_grad = lax.dot_general(flat_rows, scaled, (((0,), (0,)), ((), ())), preferred_element_type=jnp.float32)
    grad_queries, grad_keys, grad_values = attend_back(queries, keys_all, values_all, probs, grad_attended)
    grad_packed = jnp.stack([grad_queries, grad_keys, grad_values], 2)
    grad_packed = grad_packed.reshape(batch_count * length, 3 * inner_width).astype(jnp.bfloat16)
    grad_modulated = lax.dot_general(grad_packed, project, (((1,), (1,)), ((), ())), preferred_element_type=jnp.float32)
    grad_modulated = grad_modulated.reshape(batch_count, length, model_width)
    grad_in = grad_out.astype(jnp.float32) + modulate_back(grad_modulated, normed, inverse_std, scale_row)
    return (grad_in, merge_grad)

def reference(tokens, modulation, spatial_project, spatial_merge, temporal_project, temporal_merge, cotangent):

    def clip_pass(inputs):
        tile, conditioning, incoming = inputs
        spatial_in = tile.reshape(FRAMES, PATCHES, D)
        middle, saved_space = block_forward(spatial_in, spatial_project, spatial_merge, conditioning[0], conditioning[1], conditioning[2])
        temporal_in = jnp.swapaxes(middle, 0, 1)
        output, saved_time = block_forward(temporal_in, temporal_project, temporal_merge, conditioning[3], conditioning[4], conditioning[5])
        result_tile = jnp.swapaxes(output, 0, 1).reshape(FRAMES, 2, HALF, D)
        grad_time = jnp.swapaxes(incoming.reshape(FRAMES, PATCHES, D), 0, 1)
        grad_middle, merge_grad = block_backward(grad_time, temporal_project, temporal_merge, conditioning[4], conditioning[5], saved_time)
        grad_middle = jnp.swapaxes(grad_middle, 0, 1).astype(jnp.bfloat16)
        grad_tokens, unused_grad = block_backward(grad_middle, spatial_project, spatial_merge, conditioning[1], conditioning[2], saved_space)
        grad_tokens = grad_tokens.astype(jnp.bfloat16).reshape(2 * FRAMES, HALF, D)
        return (result_tile, grad_tokens, merge_grad)
    result, token_grads, merge_stack = lax.map(clip_pass, (tokens, modulation, cotangent))
    return (result, token_grads, lax.optimization_barrier(jnp.sum(merge_stack, 0)))
```

```python
import jax
import jax.numpy as jnp
from jax import lax
from jax.experimental import pallas as pl
from jax.experimental.pallas import tpu as pltpu
from jax.sharding import PartitionSpec as P

HEAD_DIM = 72
MESH = pl.DeviceIdType.MESH
LOW, RING = 4, 8
TILE = (16, 128)


class Place:
    def __init__(self):
        outer = lax.axis_index("dp")
        inner = lax.axis_index("seq")
        self.core = lax.rem(outer, 2)
        self.high = lax.rem(lax.div(outer, 2), 2)
        self.x = lax.div(outer, 4)
        self.low = lax.div(inner, RING)
        self.y = lax.rem(inner, RING)
        self.z = self.high * LOW + self.low
        self.way = 1 - 2 * self.core

    def low_at(self, step):
        return lax.rem(self.low + step + LOW, LOW)

    def y_at(self, step):
        return lax.rem(self.y + step + RING, RING)

    def device(self, x=None, y=None, z=None, core=None):
        x = self.x if x is None else x
        y = self.y if y is None else y
        z = self.z if z is None else z
        core = self.core if core is None else core
        outer = (x * 2 + lax.div(z, LOW)) * 2 + core
        return (outer, lax.rem(z, LOW) * RING + y)

    def y_to(self, step):
        return self.device(y=self.y_at(step))

    def z_to(self, step):
        return self.device(z=lax.rem(self.z + step + RING, RING))

    def sibling(self):
        return self.device(core=1 - self.core)


def greet(devices):
    barrier = pltpu.get_barrier_semaphore()
    for device in devices:
        pl.semaphore_signal(barrier, inc=1, device_id=device, device_id_type=MESH)
    pl.semaphore_wait(barrier, len(devices))


class Link:
    def __init__(self, send_sems, recv_sems):
        self.send_sems, self.recv_sems = send_sems, recv_sems
        self.count = 0
        self.started = []

    def number(self):
        self.count += 1
        return self.count - 1

    def copy(self, number, source, target, device):
        return pltpu.make_async_remote_copy(
            src_ref=source,
            dst_ref=target,
            send_sem=self.send_sems.at[number],
            recv_sem=self.recv_sems.at[number],
            device_id=device,
            device_id_type=MESH,
        )

    def send(self, source, target, device):
        number = self.number()
        copy = self.copy(number, source, target, device)
        copy.start()
        self.started.append(copy)
        return number

    def arrived(self, number, target, device):
        self.copy(number, target, target, device).wait_recv()

    def finish(self):
        for copy in self.started:
            copy.wait_send()
        self.started = []


def gather_y_first(place, link, held, first, other, count):
    way = place.way
    up, down = place.y_to(1), place.y_to(-1)
    above, below = place.z_to(1), place.z_to(-1)
    sibling = place.sibling()

    def one(step):
        return held.at[place.low, place.y_at(step), pl.ds(first, count)]

    def ring(step, start):
        return held.at[place.low_at(step), :, pl.ds(start, count)]

    def go(ref, device):
        return link.send(ref, ref, device)

    plus, minus = go(one(0), up), go(one(0), down)
    yield
    for step in (1, 2):
        link.arrived(plus, one(-step), up)
        plus = go(one(-step), up)
        link.arrived(minus, one(step), down)
        minus = go(one(step), down)
        yield
    link.arrived(plus, one(-3), up)
    link.arrived(minus, one(3), down)
    last = go(one(-3 * way), place.y_to(way))
    yield
    link.arrived(last, one(4), up)
    plus, minus = go(ring(0, first), above), go(ring(0, first), below)
    shared = [(go(ring(0, first), sibling), 0)]
    yield
    link.arrived(plus, ring(-1, first), above)
    link.arrived(minus, ring(1, first), below)
    last = go(ring(-way, first), place.z_to(way))
    shared.append((go(ring(-1, first), sibling), -1))
    shared.append((go(ring(1, first), sibling), 1))
    yield
    link.arrived(last, ring(2, first), above)
    shared.append((go(ring(2, first), sibling), 2))
    yield
    for number, step in shared:
        link.arrived(number, ring(step, other), sibling)
    yield


def gather_z_first(place, link, held, first, other, count):
    way = place.way
    up, down = place.y_to(1), place.y_to(-1)
    above, below = place.z_to(1), place.z_to(-1)
    sibling = place.sibling()

    def one(step):
        return held.at[place.low_at(step), place.y, pl.ds(first, count)]

    def run(step, start):
        return held.at[:, place.y_at(step), pl.ds(start, count)]

    def go(ref, device):
        return link.send(ref, ref, device)

    plus, minus = go(one(0), above), go(one(0), below)
    yield
    link.arrived(plus, one(-1), above)
    link.arrived(minus, one(1), below)
    last = go(one(-way), place.z_to(way))
    yield
    link.arrived(last, one(2), above)
    plus, minus = go(run(0, first), up), go(run(0, first), down)
    shared = [(go(run(0, first), sibling), 0)]
    yield
    for step in (1, 2):
        link.arrived(plus, run(-step, first), up)
        plus = go(run(-step, first), up)
        link.arrived(minus, run(step, first), down)
        minus = go(run(step, first), down)
        shared.append((go(run(-step, first), sibling), -step))
        shared.append((go(run(step, first), sibling), step))
        yield
    link.arrived(plus, run(-3, first), up)
    link.arrived(minus, run(3, first), down)
    last = go(run(-3 * way, first), place.y_to(way))
    shared.append((go(run(-3, first), sibling), -3))
    shared.append((go(run(3, first), sibling), 3))
    yield
    link.arrived(last, run(4, first), up)
    shared.append((go(run(4, first), sibling), 4))
    yield
    for number, step in shared:
        link.arrived(number, run(step, other), sibling)
    yield


def gather(place, link, held, begin, y_count, z_count):
    half = y_count + z_count
    mine, other = begin + place.core * half, begin + (1 - place.core) * half
    plans = [
        gather_y_first(place, link, held, mine, other, y_count),
        gather_z_first(place, link, held, mine + y_count, other + y_count, z_count),
    ]
    while plans:
        for plan in list(plans):
            if next(plan, plans) is plans:
                plans.remove(plan)
        yield


def lane_tiles(width):
    return [(at, min(128, width - at)) for at in range(0, width, 128)]


def pack_own(shard, staged, wide, local, begin):
    rows, width = shard.shape
    full, rest = rows // 16, rows % 16
    tiles = lane_tiles(width)
    number = begin
    for block in range(full):
        for at, lanes in tiles:
            local[number, :, :lanes] = shard[16 * block : 16 * block + 16, at : at + lanes]
            number += 1
    per = 16 // rest
    wide[:rest, :width] = shard[16 * full :, :].astype(jnp.float32)
    groups = -(-len(tiles) // per)
    for index, (at, lanes) in enumerate(tiles):
        staged[index // per, pl.ds(rest * (index % per), rest), :lanes] = wide[
            :rest, at : at + lanes
        ]
    for group in range(groups):
        local[number + group] = staged[group].astype(jnp.bfloat16)


def hold_own(place, local, held, begin, count):
    mine = pl.ds(begin + place.core * (count // 2), count // 2)
    held[place.low, place.y, mine] = local[mine]


def unpack_all(held, begin, rows, width, stage, out):
    full, rest = rows // 16, rows % 16
    tiles = lane_tiles(width)
    per = 16 // rest
    several = 4 if rows == 36 else 8
    block = several * rows

    def step(index, carry):
        low, y = lax.div(index * several, RING), lax.rem(index * several, RING)
        for shard in range(several):
            top = shard * rows
            for part in range(full):
                for tile, (at, lanes) in enumerate(tiles):
                    value = held[low, y + shard, begin + part * len(tiles) + tile]
                    stage[top + 16 * part : top + 16 * part + 16, at : at + lanes] = value.astype(
                        jnp.float32
                    )[:, :lanes]
            for group in range(-(-len(tiles) // per)):
                value = held[low, y + shard, begin + full * len(tiles) + group]
                value = value.astype(jnp.float32)
                for piece in range(per):
                    tile = group * per + piece
                    if tile < len(tiles):
                        at, lanes = tiles[tile]
                        stage[top + 16 * full : top + rows, at : at + lanes] = value[
                            rest * piece : rest * piece + rest, :lanes
                        ]
        out[pl.ds(pl.multiple_of(index * block, 16), block), :] = stage[:block, :width].astype(
            jnp.bfloat16
        )
        return carry

    lax.fori_loop(0, 32 // several, step, 0)


PROJECT_TILES, MERGE_TILES = 32, 12
HELD_TILES = 2 * (PROJECT_TILES + MERGE_TILES)
GATHER_COPIES = 32


def gather_kernel(
    space_project,
    space_merge,
    time_project,
    time_merge,
    space_project_all,
    space_merge_all,
    time_project_all,
    time_merge_all,
    held,
    staged,
    wide,
    stage,
    local,
    send_sems,
    recv_sems,
):
    place = Place()
    greet(
        [place.y_to(1), place.y_to(-1), place.z_to(1), place.z_to(-1), place.sibling()]
    )
    starts = (0, PROJECT_TILES, PROJECT_TILES + MERGE_TILES, 2 * PROJECT_TILES + MERGE_TILES)
    shards = (space_project, space_merge, time_project, time_merge)
    links = [Link(send_sems.at[i], recv_sems.at[i]) for i in range(3)]
    pack_own(space_project, staged, wide, local, starts[0])
    hold_own(place, local, held, starts[0], 32)
    plans = [gather(place, links[0], held, 0, 9, 7)]
    next(plans[0])
    for shard, start in zip(shards[1:], starts[1:]):
        pack_own(shard, staged, wide, local, start)
    hold_own(place, local, held, starts[1], 12)
    hold_own(place, local, held, starts[2], 44)
    plans.append(gather(place, links[1], held, starts[1], 4, 2))
    plans.append(gather(place, links[2], held, starts[2], 13, 9))
    live = list(plans)
    while live:
        for plan in list(live):
            if next(plan, live) is live:
                live.remove(plan)
    unpack_all(held, starts[0], 36, 1728, stage, space_project_all)
    unpack_all(held, starts[1], 18, 1152, stage, space_merge_all)
    unpack_all(held, starts[2], 36, 1728, stage, time_project_all)
    unpack_all(held, starts[3], 18, 1152, stage, time_merge_all)
    for link in links:
        link.finish()


def gather_weights(space_project, space_merge, time_project, time_merge):
    vmem = pl.BlockSpec(memory_space=pltpu.VMEM)
    project = jax.ShapeDtypeStruct((1152, 1728), jnp.bfloat16)
    merge = jax.ShapeDtypeStruct((576, 1152), jnp.bfloat16)
    return pl.pallas_call(
        gather_kernel,
        out_shape=[project, merge, project, merge],
        in_specs=[vmem] * 4,
        out_specs=[vmem] * 4,
        scratch_shapes=[
            pltpu.VMEM((LOW, RING, HELD_TILES) + TILE, jnp.bfloat16),
            pltpu.VMEM((4,) + TILE, jnp.float32),
            pltpu.VMEM((8, 1792), jnp.float32),
            pltpu.VMEM((144, 1792), jnp.float32),
            pltpu.VMEM((HELD_TILES,) + TILE, jnp.bfloat16),
            pltpu.SemaphoreType.DMA((3, GATHER_COPIES)),
            pltpu.SemaphoreType.DMA((3, GATHER_COPIES)),
        ],
        compiler_params=pltpu.CompilerParams(
            collective_id=0, has_side_effects=True, vmem_limit_bytes=56 * 1024 * 1024
        ),
        cost_estimate=pl.CostEstimate(flops=0, bytes_accessed=22_000_000, transcendentals=0),
        name="gather_weights",
    )(space_project, space_merge, time_project, time_merge)


REDUCE_COPIES = 16


def reduce_plan(place, link, packed, near, total, long_out, long_in, short_out, short_in, small, final):
    way, half = place.way, MERGE_TILES // 2
    mine, other = place.core * half, (1 - place.core) * half
    sibling = place.sibling()
    number = link.send(packed.at[:, :, pl.ds(other, half)], near, sibling)
    yield
    link.arrived(number, near, sibling)

    def add(low, carry):
        for y in range(RING):
            total[low, y] = packed[low, y, pl.ds(mine, half)].astype(jnp.float32) + near[
                low, y
            ].astype(jnp.float32)
        return carry

    lax.fori_loop(0, LOW, add, 0)
    there, back = place.y_to(way), place.y_to(-way)
    for step in range(4):
        value = total[:, place.y_at((4 - step) * way)]
        if step:
            link.arrived(long_number, long_in.at[step - 1], there)
            value = value + long_in[step - 1].astype(jnp.float32)
        long_out[step] = value.astype(jnp.bfloat16)
        long_number = link.send(long_out.at[step], long_in.at[step], there)
        if step < 3:
            value = total[:, place.y_at((step - 3) * way)]
            if step:
                link.arrived(short_number, short_in.at[step - 1], back)
                value = value + short_in[step - 1].astype(jnp.float32)
            short_out[step] = value.astype(jnp.bfloat16)
            short_number = link.send(short_out.at[step], short_in.at[step], back)
        yield
    link.arrived(short_number, short_in.at[2], back)
    link.arrived(long_number, long_in.at[3], there)
    small[pl.ds(0, 4)] = (
        total[:, place.y] + long_in[3].astype(jnp.float32) + short_in[2].astype(jnp.float32)
    )
    parity, upper = lax.rem(place.low, 2), lax.div(place.low, 2)
    device = place.device(z=place.z + 1 - 2 * parity)
    numbers = [
        link.send(small.at[1 - parity + 2 * k], small.at[4 + k], device) for k in range(2)
    ]
    yield
    for k in range(2):
        link.arrived(numbers[k], small.at[4 + k], device)
        small[6 + k] = small[parity + 2 * k] + small[4 + k]
    device = place.device(z=place.z + 2 - 4 * upper)
    number = link.send(small.at[7 - upper], small.at[8], device)
    yield
    link.arrived(number, small.at[8], device)
    small[9] = small[6 + upper] + small[8]
    at = 9
    for device in (
        place.device(z=lax.rem(place.z + LOW, RING)),
        place.device(x=place.x + 1 - 2 * lax.rem(place.x, 2)),
        place.device(x=lax.rem(place.x + 2, 4)),
    ):
        number = link.send(small.at[at], small.at[at + 1], device)
        yield
        link.arrived(number, small.at[at + 1], device)
        small[at + 2] = small[at] + small[at + 1]
        at += 2
    final[pl.ds(mine, half)] = small[at]
    number = link.send(final.at[pl.ds(mine, half)], final.at[pl.ds(mine, half)], sibling)
    yield
    link.arrived(number, final.at[pl.ds(other, half)], sibling)


def reduce_partners(place):
    parity, upper = lax.rem(place.low, 2), lax.div(place.low, 2)
    return [
        place.sibling(),
        place.y_to(1),
        place.y_to(-1),
        place.device(z=place.z + 1 - 2 * parity),
        place.device(z=place.z + 2 - 4 * upper),
        place.device(z=lax.rem(place.z + LOW, RING)),
        place.device(x=place.x + 1 - 2 * lax.rem(place.x, 2)),
        place.device(x=lax.rem(place.x + 2, 4)),
    ]


def pack_partial(part, stage, staged, packed):
    def step(low, carry):
        stage[...] = part[pl.ds(pl.multiple_of(low * 144, 16), 144), :].astype(jnp.float32)
        staged[...] = jnp.zeros_like(staged)
        for y in range(RING):
            for tile in range(9):
                at = 128 * tile
                packed[low, y, tile] = stage[18 * y : 18 * y + 16, at : at + 128].astype(
                    jnp.bfloat16
                )
                staged[y, tile // 8, 2 * (tile % 8) : 2 * (tile % 8) + 2, :] = stage[
                    18 * y + 16 : 18 * y + 18, at : at + 128
                ]
            for group in range(3):
                packed[low, y, 9 + group] = staged[y, group].astype(jnp.bfloat16)
        return carry

    lax.fori_loop(0, LOW, step, 0)


def unpack_final(final, out):
    for tile in range(9):
        at = 128 * tile
        out[0:16, at : at + 128] = final[tile]
        out[16:18, at : at + 128] = final[9 + tile // 8, 2 * (tile % 8) : 2 * (tile % 8) + 2, :]


def reduce_kernel(
    part, out, stage, staged, packed, near, total, long_out, long_in, short_out, short_in, small,
    final, send_sems, recv_sems,
):
    place = Place()
    greet(reduce_partners(place))
    link = Link(send_sems, recv_sems)
    pack_partial(part, stage, staged, packed)
    for _ in reduce_plan(
        place, link, packed, near, total, long_out, long_in, short_out, short_in, small, final
    ):
        pass
    unpack_final(final, out)
    link.finish()


def reduce_scratch():
    half = MERGE_TILES // 2
    return [
        pltpu.VMEM((144, 1152), jnp.float32),
        pltpu.VMEM((RING, 3) + TILE, jnp.float32),
        pltpu.VMEM((LOW, RING, MERGE_TILES) + TILE, jnp.bfloat16),
        pltpu.VMEM((LOW, RING, half) + TILE, jnp.bfloat16),
        pltpu.VMEM((LOW, RING, half) + TILE, jnp.float32),
        pltpu.VMEM((4, LOW, half) + TILE, jnp.bfloat16),
        pltpu.VMEM((4, LOW, half) + TILE, jnp.bfloat16),
        pltpu.VMEM((3, LOW, half) + TILE, jnp.bfloat16),
        pltpu.VMEM((3, LOW, half) + TILE, jnp.bfloat16),
        pltpu.VMEM((16, half) + TILE, jnp.float32),
        pltpu.VMEM((MERGE_TILES,) + TILE, jnp.float32),
        pltpu.SemaphoreType.DMA((REDUCE_COPIES,)),
        pltpu.SemaphoreType.DMA((REDUCE_COPIES,)),
    ]


def reduce_grads(part):
    vmem = pl.BlockSpec(memory_space=pltpu.VMEM)
    return pl.pallas_call(
        reduce_kernel,
        out_shape=jax.ShapeDtypeStruct((18, 1152), jnp.float32),
        in_specs=[vmem],
        out_specs=vmem,
        scratch_shapes=reduce_scratch(),
        compiler_params=pltpu.CompilerParams(
            collective_id=1, has_side_effects=True, vmem_limit_bytes=56 * 1024 * 1024
        ),
        cost_estimate=pl.CostEstimate(flops=0, bytes_accessed=8_000_000, transcendentals=0),
        name="reduce_grads",
    )(part)


EPSILON = 1e-06
SPATIAL_FORMS = ("qhe,khe->hqk", "hqk,khe->qhe", "hqk,qhe->khe")
TEMPORAL_FORMS = ("fphe,gphe->phfg", "phfg,gphe->fphe", "phfg,fphe->gphe")


def swapped(array, axis, bit):
    return lax.ppermute(array, axis, [(i, i ^ 1 << bit) for i in range(lax.axis_size(axis))])


def modulate(tokens_in, shift_row, scale_row):
    widened = tokens_in.astype(jnp.float32)
    average = jnp.mean(widened, -1, keepdims=True)
    centered = widened - average
    variance = jnp.mean(centered * centered, -1, keepdims=True)
    inverse_std = lax.rsqrt(variance + EPSILON)
    normed = centered * inverse_std
    modulated = (normed * (1.0 + scale_row) + shift_row).astype(jnp.bfloat16)
    return (modulated, normed, inverse_std)


def modulate_back(grad_modulated, normed, inverse_std, scale_row):
    grad_normed = grad_modulated * (1.0 + scale_row)
    first_mean = jnp.mean(grad_normed, -1, keepdims=True)
    second_mean = jnp.mean(grad_normed * normed, -1, keepdims=True)
    return inverse_std * (grad_normed - first_mean - normed * second_mean)


def attend(queries, keys_all, values_all, forms):
    factor = HEAD_DIM ** (-0.5)
    scores = jnp.einsum(forms[0], queries, keys_all, preferred_element_type=jnp.float32) * factor
    probs = jax.nn.softmax(scores, -1)
    weights16 = probs.astype(jnp.bfloat16)
    attended = jnp.einsum(forms[1], weights16, values_all, preferred_element_type=jnp.float32)
    return (attended.astype(jnp.bfloat16), probs)


def attend_back(queries, keys_all, values_all, probs, grad_attended, forms):
    factor = HEAD_DIM ** (-0.5)
    weights16 = probs.astype(jnp.bfloat16)
    grad_probs = jnp.einsum(forms[0], grad_attended, values_all, preferred_element_type=jnp.float32)
    grad_values = jnp.einsum(forms[2], weights16, grad_attended, preferred_element_type=jnp.float32)
    totals = jnp.sum(probs * grad_probs, -1, keepdims=True)
    grad_scores = (probs * (grad_probs - totals) * factor).astype(jnp.bfloat16)
    grad_queries = jnp.einsum(forms[1], grad_scores, keys_all, preferred_element_type=jnp.float32)
    grad_keys = jnp.einsum(forms[2], grad_scores, queries, preferred_element_type=jnp.float32)
    return (grad_queries, grad_keys, grad_values)


def contract_rows(left, right):
    return lax.dot_general(
        left, right, (((1,), (1,)), ((), ())), preferred_element_type=jnp.float32
    )


def body(
    tokens, modulation, spatial_project, spatial_merge, temporal_project, temporal_merge, cotangent
):
    members = lax.axis_size("seq")
    conditioning = modulation[0]
    inner_width = spatial_merge.shape[0] * members
    head_count = inner_width // HEAD_DIM
    space_project, space_merge, time_project, time_merge = gather_weights(
        spatial_project, spatial_merge, temporal_project, temporal_merge
    )
    local_tokens = tokens[0, 0]
    token_count, model_width = local_tokens.shape
    block_rows = token_count // members
    modulated, normed_space, inverse_space = modulate(
        local_tokens, conditioning[0], conditioning[1]
    )
    packed = jnp.dot(modulated, space_project, preferred_element_type=jnp.float32).astype(
        jnp.bfloat16
    )
    far_pairs = swapped(packed[:, inner_width:], "seq", 0)
    queries = packed[:, :inner_width].reshape(token_count, head_count, HEAD_DIM)
    keys_all = jnp.concatenate(
        [packed[:, inner_width : 2 * inner_width], far_pairs[:, :inner_width]], 0
    )
    keys_all = keys_all.reshape(2 * token_count, head_count, HEAD_DIM)
    values_all = jnp.concatenate([packed[:, 2 * inner_width :], far_pairs[:, inner_width:]], 0)
    values_all = values_all.reshape(2 * token_count, head_count, HEAD_DIM)
    attended, space_probs = attend(queries, keys_all, values_all, SPATIAL_FORMS)
    flat_space = attended.reshape(token_count, inner_width)
    branch = jnp.dot(flat_space, space_merge, preferred_element_type=jnp.float32)
    middle = (local_tokens.astype(jnp.float32) + conditioning[2] * branch).astype(jnp.bfloat16)
    moved = lax.all_to_all(
        middle.reshape(members, block_rows, model_width),
        "seq",
        split_axis=0,
        concat_axis=0,
        tiled=True,
    )
    frame_count = members // 2
    across = moved.reshape(frame_count, 2 * block_rows, model_width)
    patch_count = 2 * block_rows
    modulated_time, normed_time, inverse_time = modulate(across, conditioning[3], conditioning[4])
    packed_time = jnp.dot(
        modulated_time.reshape(token_count, model_width),
        time_project,
        preferred_element_type=jnp.float32,
    ).astype(jnp.bfloat16)
    packed_time = packed_time.reshape(frame_count, patch_count, 3, head_count, HEAD_DIM)
    time_queries, time_keys, time_values = (
        packed_time[:, :, 0],
        packed_time[:, :, 1],
        packed_time[:, :, 2],
    )
    attended_time, time_probs = attend(time_queries, time_keys, time_values, TEMPORAL_FORMS)
    flat_time = attended_time.reshape(token_count, inner_width)
    branch_time = jnp.dot(flat_time, time_merge, preferred_element_type=jnp.float32)
    branch_time = branch_time.reshape(frame_count, patch_count, model_width)
    output = (across.astype(jnp.float32) + conditioning[5] * branch_time).astype(jnp.bfloat16)
    result = output.reshape(1, frame_count, 2, block_rows, model_width)
    grad_result = cotangent[0].reshape(frame_count, patch_count, model_width)
    scaled_time = (conditioning[5] * grad_result.astype(jnp.float32)).astype(jnp.bfloat16)
    scaled_time = scaled_time.reshape(token_count, model_width)
    grad_flat_time = contract_rows(scaled_time, time_merge).astype(jnp.bfloat16)
    merge_grads = reduce_grads(
        lax.dot_general(
            flat_time, scaled_time, (((0,), (0,)), ((), ())), preferred_element_type=jnp.float32
        ).astype(jnp.bfloat16)
    )
    grad_tq, grad_tk, grad_tv = attend_back(
        time_queries,
        time_keys,
        time_values,
        time_probs,
        grad_flat_time.reshape(frame_count, patch_count, head_count, HEAD_DIM),
        TEMPORAL_FORMS,
    )
    grad_packed_time = jnp.stack([grad_tq, grad_tk, grad_tv], 2).reshape(
        token_count, 3 * inner_width
    )
    grad_modulated_time = contract_rows(grad_packed_time.astype(jnp.bfloat16), time_project)
    grad_modulated_time = grad_modulated_time.reshape(frame_count, patch_count, model_width)
    grad_middle = (
        grad_result.astype(jnp.float32)
        + modulate_back(grad_modulated_time, normed_time, inverse_time, conditioning[4])
    ).astype(jnp.bfloat16)
    returned = lax.all_to_all(
        grad_middle.reshape(members, block_rows, model_width),
        "seq",
        split_axis=0,
        concat_axis=0,
        tiled=True,
    )
    returned = returned.reshape(token_count, model_width)
    scaled_space = (conditioning[2] * returned.astype(jnp.float32)).astype(jnp.bfloat16)
    grad_flat_space = contract_rows(scaled_space, space_merge).astype(jnp.bfloat16)
    grad_sq, grad_keys_all, grad_values_all = attend_back(
        queries,
        keys_all,
        values_all,
        space_probs,
        grad_flat_space.reshape(token_count, head_count, HEAD_DIM),
        SPATIAL_FORMS,
    )
    far_part = jnp.concatenate(
        [
            grad_keys_all[token_count:].reshape(token_count, inner_width),
            grad_values_all[token_count:].reshape(token_count, inner_width),
        ],
        1,
    )
    far_grads = swapped(far_part.astype(jnp.bfloat16), "seq", 0).astype(far_part.dtype)
    grad_keys = (
        grad_keys_all[:token_count].reshape(token_count, inner_width) + far_grads[:, :inner_width]
    )
    grad_values = (
        grad_values_all[:token_count].reshape(token_count, inner_width) + far_grads[:, inner_width:]
    )
    grad_packed = jnp.concatenate(
        [grad_sq.reshape(token_count, inner_width), grad_keys, grad_values], 1
    )
    grad_modulated = contract_rows(grad_packed.astype(jnp.bfloat16), space_project)
    grad_tokens = (
        returned.astype(jnp.float32)
        + modulate_back(grad_modulated, normed_space, inverse_space, conditioning[1])
    ).astype(jnp.bfloat16)
    return (result, grad_tokens.reshape(1, 1, token_count, model_width), merge_grads)


def solution(mesh):
    in_specs = (
        P("dp", "seq", None, None),
        P("dp", None, None),
        P("seq", None),
        P("seq", None),
        P("seq", None),
        P("seq", None),
        P("dp", None, None, "seq", None),
    )
    out_specs = (P("dp", None, None, "seq", None), P("dp", "seq", None, None), P("seq", None))
    return jax.shard_map(body, mesh=mesh, in_specs=in_specs, out_specs=out_specs, check_vma=False)
```

```python
import jax
import jax.numpy as jnp
from jax import lax
from jax.experimental import pallas as pl
from jax.experimental.pallas import tpu as pltpu
from jax.sharding import PartitionSpec as P

HEAD_DIM = 72
MESH = pl.DeviceIdType.MESH
LOW, RING = 4, 8
TILE = (16, 128)


class Place:
    def __init__(self):
        outer = lax.axis_index("dp")
        inner = lax.axis_index("seq")
        self.core = lax.rem(outer, 2)
        self.high = lax.rem(lax.div(outer, 2), 2)
        self.x = lax.div(outer, 4)
        self.low = lax.div(inner, RING)
        self.y = lax.rem(inner, RING)
        self.z = self.high * LOW + self.low
        self.way = 1 - 2 * self.core

    def low_at(self, step):
        return lax.rem(self.low + step + LOW, LOW)

    def y_at(self, step):
        return lax.rem(self.y + step + RING, RING)

    def device(self, x=None, y=None, z=None, core=None):
        x = self.x if x is None else x
        y = self.y if y is None else y
        z = self.z if z is None else z
        core = self.core if core is None else core
        outer = (x * 2 + lax.div(z, LOW)) * 2 + core
        return (outer, lax.rem(z, LOW) * RING + y)

    def y_to(self, step):
        return self.device(y=self.y_at(step))

    def z_to(self, step):
        return self.device(z=lax.rem(self.z + step + RING, RING))

    def sibling(self):
        return self.device(core=1 - self.core)


def greet(devices):
    barrier = pltpu.get_barrier_semaphore()
    for device in devices:
        pl.semaphore_signal(barrier, inc=1, device_id=device, device_id_type=MESH)
    return len(devices)


class Link:
    def __init__(self, send_sems, recv_sems):
        self.send_sems, self.recv_sems = send_sems, recv_sems
        self.count = 0
        self.started = []

    def number(self):
        self.count += 1
        return self.count - 1

    def copy(self, number, source, target, device):
        return pltpu.make_async_remote_copy(
            src_ref=source,
            dst_ref=target,
            send_sem=self.send_sems.at[number],
            recv_sem=self.recv_sems.at[number],
            device_id=device,
            device_id_type=MESH,
        )

    def send(self, source, target, device):
        number = self.number()
        copy = self.copy(number, source, target, device)
        copy.start()
        self.started.append(copy)
        return number

    def arrived(self, number, target, device):
        self.copy(number, target, target, device).wait_recv()

    def finish(self):
        for copy in self.started:
            copy.wait_send()
        self.started = []


def gather_y_first(place, link, held, first, other, count):
    way = place.way
    up, down = place.y_to(1), place.y_to(-1)
    above, below = place.z_to(1), place.z_to(-1)
    sibling = place.sibling()

    def one(step):
        return held.at[place.low, place.y_at(step), pl.ds(first, count)]

    def ring(step, start):
        return held.at[place.low_at(step), :, pl.ds(start, count)]

    def go(ref, device):
        return link.send(ref, ref, device)

    plus, minus = go(one(0), up), go(one(0), down)
    yield
    for step in (1, 2):
        link.arrived(plus, one(-step), up)
        plus = go(one(-step), up)
        link.arrived(minus, one(step), down)
        minus = go(one(step), down)
        yield
    link.arrived(plus, one(-3), up)
    link.arrived(minus, one(3), down)
    last = go(one(-3 * way), place.y_to(way))
    yield
    link.arrived(last, one(4), up)
    plus, minus = go(ring(0, first), above), go(ring(0, first), below)
    shared = [(go(ring(0, first), sibling), 0)]
    yield
    link.arrived(plus, ring(-1, first), above)
    link.arrived(minus, ring(1, first), below)
    last = go(ring(-way, first), place.z_to(way))
    shared.append((go(ring(-1, first), sibling), -1))
    shared.append((go(ring(1, first), sibling), 1))
    yield
    link.arrived(last, ring(2, first), above)
    shared.append((go(ring(2, first), sibling), 2))
    yield
    for number, step in shared:
        link.arrived(number, ring(step, other), sibling)
    yield


def gather_z_first(place, link, held, first, other, count):
    way = place.way
    up, down = place.y_to(1), place.y_to(-1)
    above, below = place.z_to(1), place.z_to(-1)
    sibling = place.sibling()

    def one(step):
        return held.at[place.low_at(step), place.y, pl.ds(first, count)]

    def run(step, start):
        return held.at[:, place.y_at(step), pl.ds(start, count)]

    def go(ref, device):
        return link.send(ref, ref, device)

    plus, minus = go(one(0), above), go(one(0), below)
    yield
    link.arrived(plus, one(-1), above)
    link.arrived(minus, one(1), below)
    last = go(one(-way), place.z_to(way))
    yield
    link.arrived(last, one(2), above)
    plus, minus = go(run(0, first), up), go(run(0, first), down)
    shared = [(go(run(0, first), sibling), 0)]
    yield
    for step in (1, 2):
        link.arrived(plus, run(-step, first), up)
        plus = go(run(-step, first), up)
        link.arrived(minus, run(step, first), down)
        minus = go(run(step, first), down)
        shared.append((go(run(-step, first), sibling), -step))
        shared.append((go(run(step, first), sibling), step))
        yield
    link.arrived(plus, run(-3, first), up)
    link.arrived(minus, run(3, first), down)
    last = go(run(-3 * way, first), place.y_to(way))
    shared.append((go(run(-3, first), sibling), -3))
    shared.append((go(run(3, first), sibling), 3))
    yield
    link.arrived(last, run(4, first), up)
    shared.append((go(run(4, first), sibling), 4))
    yield
    for number, step in shared:
        link.arrived(number, run(step, other), sibling)
    yield


def gather(place, link, held, begin, y_count, z_count):
    half = y_count + z_count
    mine, other = begin + place.core * half, begin + (1 - place.core) * half
    plans = [
        gather_y_first(place, link, held, mine, other, y_count),
        gather_z_first(place, link, held, mine + y_count, other + y_count, z_count),
    ]
    while plans:
        for plan in list(plans):
            if next(plan, plans) is plans:
                plans.remove(plan)
        yield


def lane_tiles(width):
    return [(at, min(128, width - at)) for at in range(0, width, 128)]


def pack_own(shard, staged, wide, local, begin):
    rows, width = shard.shape
    full, rest = rows // 16, rows % 16
    tiles = lane_tiles(width)
    number = begin
    for block in range(full):
        for at, lanes in tiles:
            local[number, :, :lanes] = shard[16 * block : 16 * block + 16, at : at + lanes]
            number += 1
    per = 16 // rest
    wide[:rest, :width] = shard[16 * full :, :].astype(jnp.float32)
    groups = -(-len(tiles) // per)
    for index, (at, lanes) in enumerate(tiles):
        staged[index // per, pl.ds(rest * (index % per), rest), :lanes] = wide[
            :rest, at : at + lanes
        ]
    for group in range(groups):
        local[number + group] = staged[group].astype(jnp.bfloat16)


def hold_own(place, local, held, begin, count):
    mine = pl.ds(begin + place.core * (count // 2), count // 2)
    held[place.low, place.y, mine] = local[mine]


def unpack_all(held, begin, rows, width, stage, out):
    full, rest = rows // 16, rows % 16
    tiles = lane_tiles(width)
    per = 16 // rest
    several = 4 if rows == 36 else 8
    block = several * rows

    def step(index, carry):
        low, y = lax.div(index * several, RING), lax.rem(index * several, RING)
        for shard in range(several):
            top = shard * rows
            for part in range(full):
                for tile, (at, lanes) in enumerate(tiles):
                    value = held[low, y + shard, begin + part * len(tiles) + tile]
                    stage[top + 16 * part : top + 16 * part + 16, at : at + lanes] = value.astype(
                        jnp.float32
                    )[:, :lanes]
            for group in range(-(-len(tiles) // per)):
                value = held[low, y + shard, begin + full * len(tiles) + group]
                value = value.astype(jnp.float32)
                for piece in range(per):
                    tile = group * per + piece
                    if tile < len(tiles):
                        at, lanes = tiles[tile]
                        stage[top + 16 * full : top + rows, at : at + lanes] = value[
                            rest * piece : rest * piece + rest, :lanes
                        ]
        out[pl.ds(pl.multiple_of(index * block, 16), block), :] = stage[:block, :width].astype(
            jnp.bfloat16
        )
        return carry

    lax.fori_loop(0, 32 // several, step, 0)


PROJECT_TILES, MERGE_TILES = 32, 12
HELD_TILES = 2 * (PROJECT_TILES + MERGE_TILES)
GATHER_COPIES = 32
REDUCE_COPIES = 16


def reduce_plan(place, link, packed, near, total, long_out, long_in, short_out, short_in, small, final):
    way, half = place.way, MERGE_TILES // 2
    mine, other = place.core * half, (1 - place.core) * half
    sibling = place.sibling()
    number = link.send(packed.at[:, :, pl.ds(other, half)], near, sibling)
    yield
    link.arrived(number, near, sibling)

    def add(low, carry):
        for y in range(RING):
            total[low, y] = packed[low, y, pl.ds(mine, half)].astype(jnp.float32) + near[
                low, y
            ].astype(jnp.float32)
        return carry

    lax.fori_loop(0, LOW, add, 0)
    there, back = place.y_to(way), place.y_to(-way)
    for step in range(4):
        value = total[:, place.y_at((4 - step) * way)]
        if step:
            link.arrived(long_number, long_in.at[step - 1], there)
            value = value + long_in[step - 1].astype(jnp.float32)
        long_out[step] = value.astype(jnp.bfloat16)
        long_number = link.send(long_out.at[step], long_in.at[step], there)
        if step < 3:
            value = total[:, place.y_at((step - 3) * way)]
            if step:
                link.arrived(short_number, short_in.at[step - 1], back)
                value = value + short_in[step - 1].astype(jnp.float32)
            short_out[step] = value.astype(jnp.bfloat16)
            short_number = link.send(short_out.at[step], short_in.at[step], back)
        yield
    link.arrived(short_number, short_in.at[2], back)
    link.arrived(long_number, long_in.at[3], there)
    small[pl.ds(0, 4)] = (
        total[:, place.y] + long_in[3].astype(jnp.float32) + short_in[2].astype(jnp.float32)
    )
    parity, upper = lax.rem(place.low, 2), lax.div(place.low, 2)
    device = place.device(z=place.z + 1 - 2 * parity)
    numbers = [
        link.send(small.at[1 - parity + 2 * k], small.at[4 + k], device) for k in range(2)
    ]
    yield
    for k in range(2):
        link.arrived(numbers[k], small.at[4 + k], device)
        small[6 + k] = small[parity + 2 * k] + small[4 + k]
    device = place.device(z=place.z + 2 - 4 * upper)
    number = link.send(small.at[7 - upper], small.at[8], device)
    yield
    link.arrived(number, small.at[8], device)
    small[9] = small[6 + upper] + small[8]
    at = 9
    for device in (
        place.device(z=lax.rem(place.z + LOW, RING)),
        place.device(x=place.x + 1 - 2 * lax.rem(place.x, 2)),
        place.device(x=lax.rem(place.x + 2, 4)),
    ):
        number = link.send(small.at[at], small.at[at + 1], device)
        yield
        link.arrived(number, small.at[at + 1], device)
        small[at + 2] = small[at] + small[at + 1]
        at += 2
    final[pl.ds(mine, half)] = small[at]
    number = link.send(final.at[pl.ds(mine, half)], final.at[pl.ds(mine, half)], sibling)
    yield
    link.arrived(number, final.at[pl.ds(other, half)], sibling)


def pack_partial(part, stage, staged, packed):
    def step(low, carry):
        stage[...] = part[pl.ds(pl.multiple_of(low * 144, 16), 144), :].astype(jnp.float32)
        staged[...] = jnp.zeros_like(staged)
        for y in range(RING):
            for tile in range(9):
                at = 128 * tile
                packed[low, y, tile] = stage[18 * y : 18 * y + 16, at : at + 128].astype(
                    jnp.bfloat16
                )
                staged[y, tile // 8, 2 * (tile % 8) : 2 * (tile % 8) + 2, :] = stage[
                    18 * y + 16 : 18 * y + 18, at : at + 128
                ]
            for group in range(3):
                packed[low, y, 9 + group] = staged[y, group].astype(jnp.bfloat16)
        return carry

    lax.fori_loop(0, LOW, step, 0)


def unpack_final(final, out):
    for tile in range(9):
        at = 128 * tile
        out[0:16, at : at + 128] = final[tile]
        out[16:18, at : at + 128] = final[9 + tile // 8, 2 * (tile % 8) : 2 * (tile % 8) + 2, :]


MEMBERS, TOKENS, MODEL, INNER, HEADS = 32, 128, 1152, 576, 8
EPSILON = 1e-06
FACTOR = HEAD_DIM ** (-0.5)


def dot(left, right):
    return jnp.dot(left, right, preferred_element_type=jnp.float32)


def dot_lanes(left, right):
    return lax.dot_general(left, right, (((1,), (1,)), ((), ())), preferred_element_type=jnp.float32)


def dot_rows(left, right):
    return lax.dot_general(left, right, (((0,), (0,)), ((), ())), preferred_element_type=jnp.float32)


def normalize(widened):
    average = jnp.mean(widened, -1, keepdims=True)
    centered = widened - average
    variance = jnp.mean(centered * centered, -1, keepdims=True)
    inverse_std = lax.rsqrt(variance + EPSILON)
    return (centered * inverse_std, inverse_std)


def modulate_back(grad_modulated, normed, inverse_std, scale_row):
    grad_normed = grad_modulated * (1.0 + scale_row)
    first_mean = jnp.mean(grad_normed, -1, keepdims=True)
    second_mean = jnp.mean(grad_normed * normed, -1, keepdims=True)
    return inverse_std * (grad_normed - first_mean - normed * second_mean)


def head_windows():
    for head in range(HEADS):
        first = HEAD_DIM * head
        start, stop = first // 128 * 128, min(INNER, -(-(first + HEAD_DIM) // 128) * 128)
        lane = lax.broadcasted_iota(jnp.int32, (1, stop - start), 1) + start
        inside = jnp.logical_and(lane >= first, lane < first + HEAD_DIM)
        yield head, slice(start, stop), jnp.where(inside, 1.0, 0.0).astype(jnp.bfloat16)


def attend(queries, keys, values, probs_ref, attended, allowed=None):
    attended[...] = jnp.zeros_like(attended)
    for head, window, own in head_windows():
        scores = dot_lanes(queries[:, window] * own, keys[:, window]) * FACTOR
        if allowed is not None:
            scores = jnp.where(allowed, scores, -1e30)
        raised = jnp.exp(scores - jnp.max(scores, -1, keepdims=True))
        probs = raised * (1.0 / jnp.sum(raised, -1, keepdims=True))
        probs_ref[head] = probs
        attended[:, window] += dot(probs.astype(jnp.bfloat16), values[:, window] * own)


def score_grads(grad_attended, own, window, values, probs):
    grad_probs = dot_lanes(grad_attended[:, window] * own, values[:, window])
    totals = jnp.sum(probs * grad_probs, -1, keepdims=True)
    return (probs * (grad_probs - totals) * FACTOR).astype(jnp.bfloat16)


def from_blocks(blocks, wide):
    def step(pair, carry):
        rows = pl.ds(pl.multiple_of(8 * pair, 8), 8)
        wide[rows, :] = jnp.concatenate(
            [blocks[2 * pair].astype(jnp.float32), blocks[2 * pair + 1].astype(jnp.float32)], 0
        )
        return carry

    lax.fori_loop(0, MEMBERS // 2, step, 0)


def to_blocks(wide, blocks):
    def step(pair, carry):
        value = wide[pl.ds(pl.multiple_of(8 * pair, 8), 8), :]
        blocks[2 * pair] = value[:4].astype(jnp.bfloat16)
        blocks[2 * pair + 1] = value[4:].astype(jnp.bfloat16)
        return carry

    lax.fori_loop(0, MEMBERS // 2, step, 0)


def block_copy(away, source, target, sent, come, device):
    return pltpu.make_async_remote_copy(
        src_ref=source,
        dst_ref=target,
        send_sem=sent.at[away],
        recv_sem=come.at[away],
        device_id=device,
        device_id_type=MESH,
    )


def trade_start(leaving, coming, sent, come):
    outer, me = lax.axis_index("dp"), lax.axis_index("seq")

    def step(away, carry):
        there = lax.rem(me + away, MEMBERS)
        block_copy(
            away, leaving.at[there], coming.at[me], sent, come, (outer, there)
        ).start()
        return carry

    lax.fori_loop(1, MEMBERS, step, 0)
    coming[me] = leaving[me]


def trade_wait(leaving, coming, sent, come):
    outer, me = lax.axis_index("dp"), lax.axis_index("seq")

    def step(away, carry):
        there = lax.rem(me + away, MEMBERS)
        origin = lax.rem(me + MEMBERS - away, MEMBERS)
        block_copy(
            away, leaving.at[there], coming.at[origin], sent, come, (outer, there)
        ).wait()
        return carry

    lax.fori_loop(1, MEMBERS, step, 0)


def partners(place):
    outer = lax.axis_index("dp")
    me = lax.axis_index("seq")
    listed = [(outer, lax.rem(me + away, MEMBERS)) for away in range(1, MEMBERS)]
    return listed + [
        place.sibling(),
        place.z_to(1),
        place.z_to(-1),
        place.z_to(LOW),
        place.device(x=place.x + 1 - 2 * lax.rem(place.x, 2)),
        place.device(x=lax.rem(place.x + 2, 4)),
    ]


def advance(plans, rounds=1000):
    for _ in range(rounds):
        for plan in list(plans):
            if next(plan, plans) is plans:
                plans.remove(plan)
        if not plans:
            return


def split_packed(packed, rows, queries, keys, values):
    queries[...] = packed[:TOKENS, :INNER].astype(jnp.bfloat16)
    keys[...] = packed[:rows, INNER : 2 * INNER].astype(jnp.bfloat16)
    values[...] = packed[:rows, 2 * INNER : 3 * INNER].astype(jnp.bfloat16)


def scratch_table():
    f32, b16 = jnp.float32, jnp.bfloat16
    half = MERGE_TILES // 2
    project, merge = (MODEL, 3 * INNER), (INNER, MODEL)
    wide, narrow = (TOKENS, MODEL), (TOKENS, INNER)
    blocks = (MEMBERS, 4, MODEL)
    sems = pltpu.SemaphoreType.DMA
    return {
        "held": pltpu.VMEM((LOW, RING, HELD_TILES) + TILE, b16),
        "local": pltpu.VMEM((HELD_TILES,) + TILE, b16),
        "staged": pltpu.VMEM((4,) + TILE, f32),
        "loose": pltpu.VMEM((8, 1792), f32),
        "stage": pltpu.VMEM((144, 1792), f32),
        "space_project": pltpu.VMEM(project, b16),
        "space_merge": pltpu.VMEM(merge, b16),
        "time_project": pltpu.VMEM(project, b16),
        "time_merge": pltpu.VMEM(merge, b16),
        "gather_sent": sems((3, GATHER_COPIES)),
        "gather_come": sems((3, GATHER_COPIES)),
        "reduce_stage": pltpu.VMEM((144, MODEL), f32),
        "reduce_staged": pltpu.VMEM((RING, 3) + TILE, f32),
        "part": pltpu.VMEM(merge, f32),
        "packed_part": pltpu.VMEM((LOW, RING, MERGE_TILES) + TILE, b16),
        "near": pltpu.VMEM((LOW, RING, half) + TILE, b16),
        "total": pltpu.VMEM((LOW, RING, half) + TILE, f32),
        "long_out": pltpu.VMEM((4, LOW, half) + TILE, b16),
        "long_in": pltpu.VMEM((4, LOW, half) + TILE, b16),
        "short_out": pltpu.VMEM((3, LOW, half) + TILE, b16),
        "short_in": pltpu.VMEM((3, LOW, half) + TILE, b16),
        "small": pltpu.VMEM((16, half) + TILE, f32),
        "final": pltpu.VMEM((MERGE_TILES,) + TILE, f32),
        "reduce_sent": sems((REDUCE_COPIES,)),
        "reduce_come": sems((REDUCE_COPIES,)),
        "both_tokens": pltpu.VMEM((2,) + wide, b16),
        "modulated": pltpu.VMEM((2 * TOKENS, MODEL), b16),
        "packed": pltpu.VMEM((2 * TOKENS, 1792), f32),
        "space_normed": pltpu.VMEM(wide, f32),
        "space_inverse": pltpu.VMEM((TOKENS, 1), f32),
        "space_queries": pltpu.VMEM(narrow, b16),
        "space_keys": pltpu.VMEM((2 * TOKENS, INNER), b16),
        "space_values": pltpu.VMEM((2 * TOKENS, INNER), b16),
        "space_probs": pltpu.VMEM((HEADS, TOKENS, 2 * TOKENS), f32),
        "attended": pltpu.VMEM(narrow, f32),
        "time_normed": pltpu.VMEM(wide, f32),
        "time_queries": pltpu.VMEM(narrow, b16),
        "time_keys": pltpu.VMEM(narrow, b16),
        "time_values": pltpu.VMEM(narrow, b16),
        "time_probs": pltpu.VMEM((HEADS, TOKENS, TOKENS), f32),
        "wide": pltpu.VMEM(wide, f32),
        "across": pltpu.VMEM(wide, f32),
        "grad_result": pltpu.VMEM(wide, f32),
        "grad_attended": pltpu.VMEM(narrow, b16),
        "grad_scores": pltpu.VMEM((HEADS, TOKENS, 2 * TOKENS), b16),
        "grad_queries": pltpu.VMEM(narrow, f32),
        "grad_keys": pltpu.VMEM((2 * TOKENS, INNER), f32),
        "grad_values": pltpu.VMEM((2 * TOKENS, INNER), f32),
        "grad_packed": pltpu.VMEM((TOKENS, 1792), f32),
        "far_out": pltpu.VMEM((2,) + narrow, b16),
        "far_in": pltpu.VMEM((2,) + narrow, b16),
        "middle_out": pltpu.VMEM(blocks, b16),
        "middle_in": pltpu.VMEM(blocks, b16),
        "grad_out": pltpu.VMEM(blocks, b16),
        "grad_in": pltpu.VMEM(blocks, b16),
        "middle_sent": sems((MEMBERS,)),
        "middle_come": sems((MEMBERS,)),
        "grad_sent": sems((MEMBERS,)),
        "grad_come": sems((MEMBERS,)),
        "pair_sent": sems((2,)),
        "pair_come": sems((2,)),
    }


class Refs:
    def __init__(self, refs):
        for name, ref in zip(scratch_table(), refs, strict=True):
            setattr(self, name, ref)


def join_packed(grad_packed, queries, keys, values):
    grad_packed[:, :INNER] = queries
    grad_packed[:, INNER : 2 * INNER] = keys
    grad_packed[:, 2 * INNER : 3 * INNER] = values
    return grad_packed[:, : 3 * INNER].astype(jnp.bfloat16)


def clip_kernel(
    tokens,
    modulation,
    space_project,
    space_merge,
    time_project,
    time_merge,
    cotangent,
    result,
    token_grads,
    merge_grads,
    *scratch,
):
    at = Refs(scratch)
    place = Place()
    expected = greet(partners(place))

    def row(index):
        return modulation[index : index + 1, :]

    starts = (0, PROJECT_TILES, PROJECT_TILES + MERGE_TILES, 2 * PROJECT_TILES + MERGE_TILES)
    for shard, start in zip((space_project, space_merge, time_project, time_merge), starts):
        pack_own(shard, at.staged, at.loose, at.local, start)
    hold_own(place, at.local, at.held, 0, 32)
    hold_own(place, at.local, at.held, starts[1], 12)
    hold_own(place, at.local, at.held, starts[2], 44)
    at.both_tokens[0] = tokens[...]
    links = [Link(at.gather_sent.at[i], at.gather_come.at[i]) for i in range(3)]
    first = [gather(place, links[0], at.held, 0, 9, 7)]
    later = [
        gather(place, links[1], at.held, starts[1], 4, 2),
        gather(place, links[2], at.held, starts[2], 13, 9),
    ]
    pl.semaphore_wait(pltpu.get_barrier_semaphore(), expected)
    advance(first, 1)
    pair = Link(at.pair_sent, at.pair_come)
    partner = place.y_to(1 - 2 * lax.rem(place.y, 2))
    number = pair.send(at.both_tokens.at[0], at.both_tokens.at[1], partner)
    advance(first, 1)
    advance(later, 1)
    normed, inverse_std = normalize(tokens[...].astype(jnp.float32))
    at.space_normed[...] = normed
    at.space_inverse[...] = inverse_std
    at.modulated[:TOKENS] = (normed * (1.0 + row(1)) + row(0)).astype(jnp.bfloat16)
    from_blocks(cotangent, at.grad_result)
    advance(first, 1)
    pair.arrived(number, at.both_tokens.at[1], partner)
    normed, _ = normalize(at.both_tokens[1].astype(jnp.float32))
    at.modulated[TOKENS:] = (normed * (1.0 + row(1)) + row(0)).astype(jnp.bfloat16)
    while first:
        advance(first, 1)
        advance(later, 1)
    unpack_all(at.held, starts[0], 36, 1728, at.stage, at.space_project)

    at.packed[:, : 3 * INNER] = dot(at.modulated[...], at.space_project[...])
    split_packed(at.packed, 2 * TOKENS, at.space_queries, at.space_keys, at.space_values)
    advance(later, 1)
    attend(at.space_queries, at.space_keys, at.space_values, at.space_probs, at.attended)
    advance(later)
    unpack_all(at.held, starts[1], 18, 1152, at.stage, at.space_merge)
    branch = dot(at.attended[...].astype(jnp.bfloat16), at.space_merge[...])
    at.wide[...] = tokens[...].astype(jnp.float32) + row(2) * branch
    to_blocks(at.wide, at.middle_out)
    trade_start(at.middle_out, at.middle_in, at.middle_sent, at.middle_come)
    unpack_all(at.held, starts[2], 36, 1728, at.stage, at.time_project)
    unpack_all(at.held, starts[3], 18, 1152, at.stage, at.time_merge)
    scaled = (row(5) * at.grad_result[...]).astype(jnp.bfloat16)
    at.grad_attended[...] = dot_lanes(scaled, at.time_merge[...]).astype(jnp.bfloat16)
    trade_wait(at.middle_out, at.middle_in, at.middle_sent, at.middle_come)
    from_blocks(at.middle_in, at.across)

    normed, time_inverse = normalize(at.across[...])
    at.time_normed[...] = normed
    modulated = (normed * (1.0 + row(4)) + row(3)).astype(jnp.bfloat16)
    at.packed[:TOKENS, : 3 * INNER] = dot(modulated, at.time_project[...])
    split_packed(at.packed, TOKENS, at.time_queries, at.time_keys, at.time_values)
    square = (TOKENS, TOKENS)
    patch_row = lax.rem(lax.broadcasted_iota(jnp.int32, square, 0), 8)
    patch_column = lax.rem(lax.broadcasted_iota(jnp.int32, square, 1), 8)
    attend(
        at.time_queries,
        at.time_keys,
        at.time_values,
        at.time_probs,
        at.attended,
        patch_row == patch_column,
    )
    flat = at.attended[...].astype(jnp.bfloat16)
    scaled = (row(5) * at.grad_result[...]).astype(jnp.bfloat16)
    at.part[...] = dot_rows(flat, scaled)
    pack_partial(at.part, at.reduce_stage, at.reduce_staged, at.packed_part)
    reducing = Link(at.reduce_sent, at.reduce_come)
    reduction = [
        reduce_plan(
            place, reducing, at.packed_part, at.near, at.total, at.long_out, at.long_in,
            at.short_out, at.short_in, at.small, at.final,
        )
    ]
    advance(reduction, 1)
    at.wide[...] = at.across[...] + row(5) * dot(flat, at.time_merge[...])
    to_blocks(at.wide, result)
    advance(reduction, 1)

    at.grad_queries[...] = jnp.zeros_like(at.grad_queries)
    at.grad_keys[...] = jnp.zeros_like(at.grad_keys)
    at.grad_values[...] = jnp.zeros_like(at.grad_values)
    for head, window, own in head_windows():
        probs = at.time_probs[head]
        grads = score_grads(at.grad_attended, own, window, at.time_values, probs)
        at.grad_values[:TOKENS, window] += dot_rows(
            probs.astype(jnp.bfloat16), at.grad_attended[:, window] * own
        )
        at.grad_keys[:TOKENS, window] += dot_rows(grads, at.time_queries[:, window] * own)
        at.grad_queries[:, window] += dot(grads, at.time_keys[:, window] * own)
    grad_packed = join_packed(
        at.grad_packed, at.grad_queries[...], at.grad_keys[:TOKENS], at.grad_values[:TOKENS]
    )
    grad_modulated = dot_lanes(grad_packed, at.time_project[...])
    at.wide[...] = at.grad_result[...] + modulate_back(
        grad_modulated, at.time_normed[...], time_inverse, row(4)
    )
    to_blocks(at.wide, at.grad_out)
    trade_start(at.grad_out, at.grad_in, at.grad_sent, at.grad_come)
    advance(reduction, 2)
    trade_wait(at.grad_out, at.grad_in, at.grad_sent, at.grad_come)
    from_blocks(at.grad_in, at.wide)

    scaled = (row(2) * at.wide[...]).astype(jnp.bfloat16)
    at.grad_attended[...] = dot_lanes(scaled, at.space_merge[...]).astype(jnp.bfloat16)
    at.grad_keys[...] = jnp.zeros_like(at.grad_keys)
    at.grad_values[...] = jnp.zeros_like(at.grad_values)
    at.grad_queries[...] = jnp.zeros_like(at.grad_queries)
    far = pl.ds(TOKENS, TOKENS)
    for head, window, own in head_windows():
        probs = at.space_probs[head]
        grads = score_grads(at.grad_attended, own, window, at.space_values, probs)
        at.grad_scores[head] = grads
        at.grad_values[:, window] += dot_rows(
            probs.astype(jnp.bfloat16), at.grad_attended[:, window] * own
        )
        at.grad_keys[:, window] += dot_rows(grads, at.space_queries[:, window] * own)
    at.far_out[0] = at.grad_keys[far, :].astype(jnp.bfloat16)
    at.far_out[1] = at.grad_values[far, :].astype(jnp.bfloat16)
    number = pair.send(at.far_out, at.far_in, partner)
    advance(reduction, 1)
    for head, window, own in head_windows():
        at.grad_queries[:, window] += dot(at.grad_scores[head], at.space_keys[:, window] * own)
    advance(reduction, 1)
    pair.arrived(number, at.far_in, partner)
    grad_packed = join_packed(
        at.grad_packed,
        at.grad_queries[...],
        at.grad_keys[:TOKENS] + at.far_in[0].astype(jnp.float32),
        at.grad_values[:TOKENS] + at.far_in[1].astype(jnp.float32),
    )
    advance(reduction, 1)
    grad_modulated = dot_lanes(grad_packed, at.space_project[...])
    token_grads[...] = (
        at.wide[...]
        + modulate_back(grad_modulated, at.space_normed[...], at.space_inverse[...], row(1))
    ).astype(jnp.bfloat16)
    advance(reduction)
    unpack_final(at.final, merge_grads)
    for link in links + [pair, reducing]:
        link.finish()


def body(
    tokens, modulation, spatial_project, spatial_merge, temporal_project, temporal_merge, cotangent
):
    vmem = pl.BlockSpec(memory_space=pltpu.VMEM)
    blocks = (MEMBERS, 4, MODEL)
    result, token_grads, merge_grads = pl.pallas_call(
        clip_kernel,
        out_shape=[
            jax.ShapeDtypeStruct(blocks, jnp.bfloat16),
            jax.ShapeDtypeStruct((TOKENS, MODEL), jnp.bfloat16),
            jax.ShapeDtypeStruct((18, MODEL), jnp.float32),
        ],
        in_specs=[vmem] * 7,
        out_specs=[vmem] * 3,
        scratch_shapes=list(scratch_table().values()),
        compiler_params=pltpu.CompilerParams(
            collective_id=0, has_side_effects=True, vmem_limit_bytes=60 * 1024 * 1024
        ),
        cost_estimate=pl.CostEstimate(
            flops=3_000_000_000, bytes_accessed=4_000_000, transcendentals=500_000
        ),
        name="clip_step",
    )(
        tokens.reshape(TOKENS, MODEL),
        modulation.reshape(6, MODEL),
        spatial_project,
        spatial_merge,
        temporal_project,
        temporal_merge,
        cotangent.reshape(blocks),
    )
    return (
        result.reshape(1, 16, 2, 4, MODEL),
        token_grads.reshape(1, 1, TOKENS, MODEL),
        merge_grads,
    )


def solution(mesh):
    in_specs = (
        P("dp", "seq", None, None),
        P("dp", None, None),
        P("seq", None),
        P("seq", None),
        P("seq", None),
        P("seq", None),
        P("dp", None, None, "seq", None),
    )
    out_specs = (P("dp", None, None, "seq", None), P("dp", "seq", None, None), P("seq", None))
    return jax.shard_map(body, mesh=mesh, in_specs=in_specs, out_specs=out_specs, check_vma=False)
```

```python
import jax
import jax.numpy as jnp
from jax import lax
from jax.experimental import pallas as pl
from jax.experimental.pallas import tpu as pltpu
from jax.sharding import PartitionSpec as P

HEAD_DIM = 72
MESH = pl.DeviceIdType.MESH
LOW, RING = 4, 8
TILE = (16, 128)


class Place:
    def __init__(self):
        outer = lax.axis_index("dp")
        inner = lax.axis_index("seq")
        self.core = lax.rem(outer, 2)
        self.high = lax.rem(lax.div(outer, 2), 2)
        self.x = lax.div(outer, 4)
        self.low = lax.div(inner, RING)
        self.y = lax.rem(inner, RING)
        self.z = self.high * LOW + self.low
        self.way = 1 - 2 * self.core

    def low_at(self, step):
        return lax.rem(self.low + step + LOW, LOW)

    def y_at(self, step):
        return lax.rem(self.y + step + RING, RING)

    def device(self, x=None, y=None, z=None, core=None):
        x = self.x if x is None else x
        y = self.y if y is None else y
        z = self.z if z is None else z
        core = self.core if core is None else core
        outer = (x * 2 + lax.div(z, LOW)) * 2 + core
        return (outer, lax.rem(z, LOW) * RING + y)

    def y_to(self, step):
        return self.device(y=self.y_at(step))

    def x_at(self, step):
        return lax.rem(self.x + step + 4, 4)

    def x_to(self, step):
        return self.device(x=self.x_at(step))

    def z_to(self, step):
        return self.device(z=lax.rem(self.z + step + RING, RING))

    def sibling(self):
        return self.device(core=1 - self.core)


def greet(devices):
    barrier = pltpu.get_barrier_semaphore()
    for device in devices:
        pl.semaphore_signal(barrier, inc=1, device_id=device, device_id_type=MESH)
    return len(devices)


class Link:
    def __init__(self, send_sems, recv_sems):
        self.send_sems, self.recv_sems = send_sems, recv_sems
        self.count = 0
        self.started = []

    def number(self):
        self.count += 1
        return self.count - 1

    def copy(self, number, source, target, device):
        return pltpu.make_async_remote_copy(
            src_ref=source,
            dst_ref=target,
            send_sem=self.send_sems.at[number],
            recv_sem=self.recv_sems.at[number],
            device_id=device,
            device_id_type=MESH,
        )

    def send(self, source, target, device):
        number = self.number()
        copy = self.copy(number, source, target, device)
        copy.start()
        self.started.append(copy)
        return number

    def arrived(self, number, target, device):
        self.copy(number, target, target, device).wait_recv()

    def finish(self):
        for copy in self.started:
            copy.wait_send()
        self.started = []


class Gather:
    def __init__(self, place, link, held, begin, sliced, y_count, z_count):
        self.place, self.link, self.held = place, link, held
        self.begin, self.sliced = begin, sliced
        self.rest = begin + 8 * sliced
        self.y_count, self.z_count = y_count, z_count
        self.size = 8 * sliced + 2 * (y_count + z_count)

    def slice_of(self, x, core):
        return pl.ds(self.begin + (x * 2 + core) * self.sliced, self.sliced)

    def y_part(self, core):
        return pl.ds(self.rest + core * (self.y_count + self.z_count), self.y_count)

    def z_part(self, core):
        return pl.ds(
            self.rest + core * (self.y_count + self.z_count) + self.y_count, self.z_count
        )

    def hold_own(self, local):
        place, held = self.place, self.held
        for count, tiles in (
            (self.sliced, self.slice_of(place.x, place.core)),
            (self.y_count, self.y_part(place.core)),
            (self.z_count, self.z_part(place.core)),
        ):
            if count:
                held[place.low, place.y, tiles] = local[tiles]

    def go(self, ref, device):
        return self.link.send(ref, ref, device)

    def across_y(self, tiles):
        place = self.place
        return [
            (self.go(self.held.at[place.low, place.y, tiles], place.y_to(step)), step)
            for step in range(1, RING)
        ]

    def arrived_y(self, numbers, tiles):
        place = self.place
        for number, step in numbers:
            self.link.arrived(
                number, self.held.at[place.low, place.y_at(-step), tiles], place.y_to(step)
            )

    def across_z(self, part):
        place = self.place
        return [
            (self.go(part(0), place.z_to(1)), -1),
            (self.go(part(0), place.z_to(-1)), 1),
            (self.go(part(0), place.z_to(2 * place.way)), 2),
        ]

    def arrived_z(self, numbers, part):
        for number, step in numbers:
            self.link.arrived(number, part(step), self.place.z_to(1))

    def share(self, refs):
        return [self.go(ref, self.place.sibling()) for ref in refs]

    def shared(self, numbers, refs):
        for number, ref in zip(numbers, refs, strict=True):
            self.link.arrived(number, ref, self.place.sibling())

    def over_x(self):
        place, held = self.place, self.held
        mine = self.slice_of(place.x, place.core)

        def ring(step):
            return held.at[place.low_at(step), :, mine]

        def whole(step, core):
            return held.at[:, :, self.slice_of(place.x_at(step), core)]

        numbers = self.across_y(mine)
        yield
        self.arrived_y(numbers, mine)
        numbers = self.across_z(ring)
        yield
        self.arrived_z(numbers, ring)
        block = whole(0, place.core)
        plus, minus = self.go(block, place.x_to(1)), self.go(block, place.x_to(-1))
        given = self.share([block])
        yield
        self.link.arrived(plus, whole(-1, place.core), place.x_to(1))
        self.link.arrived(minus, whole(1, place.core), place.x_to(-1))
        last = self.go(whole(-place.way, place.core), place.x_to(place.way))
        given += self.share([whole(-1, place.core), whole(1, place.core)])
        yield
        self.link.arrived(last, whole(2, place.core), place.x_to(1))
        given += self.share([whole(2, place.core)])
        yield
        self.shared(given, [whole(step, 1 - place.core) for step in (0, -1, 1, 2)])
        yield

    def y_first(self):
        place, held = self.place, self.held
        mine, other = self.y_part(place.core), self.y_part(1 - place.core)

        def ring(step):
            return held.at[place.low_at(step), :, mine]

        numbers = self.across_y(mine)
        yield
        self.arrived_y(numbers, mine)
        numbers = self.across_z(ring)
        given = self.share([ring(0)])
        yield
        self.arrived_z(numbers, ring)
        given += self.share([ring(step) for step in (-1, 1, 2)])
        yield
        self.shared(given, [held.at[place.low_at(step), :, other] for step in (0, -1, 1, 2)])
        yield

    def z_first(self):
        place, held = self.place, self.held
        mine, other = self.z_part(place.core), self.z_part(1 - place.core)

        def one(step):
            return held.at[place.low_at(step), place.y, mine]

        def run(step):
            return held.at[:, place.y_at(step), mine]

        numbers = self.across_z(one)
        yield
        self.arrived_z(numbers, one)
        near = (1, -1, 2, -2)
        numbers = [self.go(run(0), place.y_to(step)) for step in near]
        given = self.share([run(0)])
        yield
        for number, step in zip(numbers, near, strict=True):
            self.link.arrived(number, run(-step), place.y_to(step))
        numbers = [
            self.go(run(-2), place.y_to(1)),
            self.go(run(2), place.y_to(-1)),
            self.go(run(-2 * place.way), place.y_to(2 * place.way)),
        ]
        given += self.share([run(-step) for step in near])
        yield
        far = (-3, 3, 4)
        for number, step in zip(numbers, far, strict=True):
            self.link.arrived(number, run(step), place.y_to(1))
        given += self.share([run(step) for step in far])
        yield
        steps = (0,) + tuple(-step for step in near) + far
        self.shared(given, [held.at[:, place.y_at(step), other] for step in steps])
        yield

    def plan(self):
        plans = [self.over_x()] if self.sliced else []
        plans += [self.z_first()] if self.z_count else []
        plans += [self.y_first()] if self.y_count else []
        while plans:
            for plan in list(plans):
                if next(plan, plans) is plans:
                    plans.remove(plan)
            yield


def lane_tiles(width):
    return [(at, min(128, width - at)) for at in range(0, width, 128)]


def pack_own(shard, staged, wide, local, begin):
    rows, width = shard.shape
    full, rest = rows // 16, rows % 16
    tiles = lane_tiles(width)
    number = begin
    for block in range(full):
        for at, lanes in tiles:
            local[number, :, :lanes] = shard[16 * block : 16 * block + 16, at : at + lanes]
            number += 1
    per = 16 // rest
    wide[:rest, :width] = shard[16 * full :, :].astype(jnp.float32)
    groups = -(-len(tiles) // per)
    for index, (at, lanes) in enumerate(tiles):
        staged[index // per, pl.ds(rest * (index % per), rest), :lanes] = wide[
            :rest, at : at + lanes
        ]
    for group in range(groups):
        local[number + group] = staged[group].astype(jnp.bfloat16)


def unpack_all(held, begin, rows, width, stage, out):
    full, rest = rows // 16, rows % 16
    tiles = lane_tiles(width)
    per = 16 // rest
    several = 4 if rows == 36 else 8
    block = several * rows

    def step(index, carry):
        low, y = lax.div(index * several, RING), lax.rem(index * several, RING)
        for shard in range(several):
            top = shard * rows
            for part in range(full):
                for tile, (at, lanes) in enumerate(tiles):
                    value = held[low, y + shard, begin + part * len(tiles) + tile]
                    stage[top + 16 * part : top + 16 * part + 16, at : at + lanes] = value.astype(
                        jnp.float32
                    )[:, :lanes]
            for group in range(-(-len(tiles) // per)):
                value = held[low, y + shard, begin + full * len(tiles) + group]
                value = value.astype(jnp.float32)
                for piece in range(per):
                    tile = group * per + piece
                    if tile < len(tiles):
                        at, lanes = tiles[tile]
                        stage[top + 16 * full : top + rows, at : at + lanes] = value[
                            rest * piece : rest * piece + rest, :lanes
                        ]
        out[pl.ds(pl.multiple_of(index * block, 16), block), :] = stage[:block, :width].astype(
            jnp.bfloat16
        )
        return carry

    lax.fori_loop(0, 32 // several, step, 0)


PROJECT_TILES, MERGE_TILES = 32, 12
HELD_TILES = 2 * (PROJECT_TILES + MERGE_TILES)
GATHER_COPIES = 52
REDUCE_COPIES = 32


Z_TILES = 4


def reduce_plan(place, link, packed, near, total, z_in, z_sum, zy_in, y_in, y_sum, yz_in, parts, final):
    half = MERGE_TILES // 2
    mine, other = place.core * half, (1 - place.core) * half
    sibling = place.sibling()
    first, second = pl.ds(0, Z_TILES), pl.ds(Z_TILES, half - Z_TILES)
    f32, b16 = jnp.float32, jnp.bfloat16
    lows = ((1, 1), (-1, -1), (2, 2 * place.way))
    number = link.send(packed.at[:, :, pl.ds(other, half)], near, sibling)
    yield
    link.arrived(number, near, sibling)

    def add(low, carry):
        for y in range(RING):
            total[low, y] = (
                packed[low, y, pl.ds(mine, half)].astype(f32) + near[low, y].astype(f32)
            ).astype(b16)
        return carry

    lax.fori_loop(0, LOW, add, 0)
    z_numbers = [
        link.send(total.at[place.low_at(step), :, first], z_in.at[slot], place.z_to(hops))
        for slot, (step, hops) in enumerate(lows)
    ]
    y_numbers = [
        link.send(total.at[:, place.y_at(step), second], y_in.at[step - 1], place.y_to(step))
        for step in range(1, RING)
    ]
    yield
    value = total[place.low, :, first].astype(f32)
    for slot, number in enumerate(z_numbers):
        link.arrived(number, z_in.at[slot], sibling)
        value = value + z_in[slot].astype(f32)
    z_sum[...] = value.astype(b16)
    z_numbers = [
        link.send(z_sum.at[place.y_at(step)], zy_in.at[step - 1], place.y_to(step))
        for step in range(1, RING)
    ]
    value = total[:, place.y, second].astype(f32)
    for slot, number in enumerate(y_numbers):
        link.arrived(number, y_in.at[slot], sibling)
        value = value + y_in[slot].astype(f32)
    y_sum[...] = value.astype(b16)
    y_numbers = [
        link.send(y_sum.at[place.low_at(step)], yz_in.at[slot], place.z_to(hops))
        for slot, (step, hops) in enumerate(lows)
    ]
    yield
    value = z_sum[place.y].astype(f32)
    for slot, number in enumerate(z_numbers):
        link.arrived(number, zy_in.at[slot], sibling)
        value = value + zy_in[slot].astype(f32)
    me = place.x * 2 + place.high
    parts[me, first] = value.astype(b16)
    value = y_sum[place.low].astype(f32)
    for slot, number in enumerate(y_numbers):
        link.arrived(number, yz_in.at[slot], sibling)
        value = value + yz_in[slot].astype(f32)
    parts[me, second] = value.astype(b16)
    numbers = []
    for step in range(1, 8):
        there = lax.rem(me + step, 8)
        device = place.device(
            x=lax.div(there, 2), z=lax.rem(there, 2) * LOW + place.low
        )
        numbers.append(link.send(parts.at[me], parts.at[me], device))
    yield
    for step, number in enumerate(numbers, 1):
        link.arrived(number, parts.at[lax.rem(me - step + 8, 8)], sibling)
    value = parts[0].astype(f32)
    for index in range(1, 8):
        value = value + parts[index].astype(f32)
    final[pl.ds(mine, half)] = value
    number = link.send(final.at[pl.ds(mine, half)], final.at[pl.ds(mine, half)], sibling)
    yield
    link.arrived(number, final.at[pl.ds(other, half)], sibling)


def pack_partial(part, stage, staged, packed):
    def step(low, carry):
        stage[...] = part[pl.ds(pl.multiple_of(low * 144, 16), 144), :].astype(jnp.float32)
        staged[...] = jnp.zeros_like(staged)
        for y in range(RING):
            for tile in range(9):
                at = 128 * tile
                packed[low, y, tile] = stage[18 * y : 18 * y + 16, at : at + 128].astype(
                    jnp.bfloat16
                )
                staged[y, tile // 8, 2 * (tile % 8) : 2 * (tile % 8) + 2, :] = stage[
                    18 * y + 16 : 18 * y + 18, at : at + 128
                ]
            for group in range(3):
                packed[low, y, 9 + group] = staged[y, group].astype(jnp.bfloat16)
        return carry

    lax.fori_loop(0, LOW, step, 0)


def unpack_final(final, out):
    for tile in range(9):
        at = 128 * tile
        out[0:16, at : at + 128] = final[tile]
        out[16:18, at : at + 128] = final[9 + tile // 8, 2 * (tile % 8) : 2 * (tile % 8) + 2, :]


MEMBERS, TOKENS, MODEL, INNER, HEADS = 32, 128, 1152, 576, 8
EPSILON = 1e-06
FACTOR = HEAD_DIM ** (-0.5)


def dot(left, right):
    return jnp.dot(left, right, preferred_element_type=jnp.float32)


def dot_lanes(left, right):
    return lax.dot_general(left, right, (((1,), (1,)), ((), ())), preferred_element_type=jnp.float32)


def dot_rows(left, right):
    return lax.dot_general(left, right, (((0,), (0,)), ((), ())), preferred_element_type=jnp.float32)


def normalize(widened):
    average = jnp.mean(widened, -1, keepdims=True)
    centered = widened - average
    variance = jnp.mean(centered * centered, -1, keepdims=True)
    inverse_std = lax.rsqrt(variance + EPSILON)
    return (centered * inverse_std, inverse_std)


def modulate_back(grad_modulated, normed, inverse_std, scale_row):
    grad_normed = grad_modulated * (1.0 + scale_row)
    first_mean = jnp.mean(grad_normed, -1, keepdims=True)
    second_mean = jnp.mean(grad_normed * normed, -1, keepdims=True)
    return inverse_std * (grad_normed - first_mean - normed * second_mean)


def head_windows():
    for head in range(HEADS):
        first = HEAD_DIM * head
        start, stop = first // 128 * 128, min(INNER, -(-(first + HEAD_DIM) // 128) * 128)
        lane = lax.broadcasted_iota(jnp.int32, (1, stop - start), 1) + start
        inside = jnp.logical_and(lane >= first, lane < first + HEAD_DIM)
        yield head, slice(start, stop), jnp.where(inside, 1.0, 0.0).astype(jnp.bfloat16)


def attend(queries, keys, values, probs_ref, attended, allowed=None):
    attended[...] = jnp.zeros_like(attended)
    for head, window, own in head_windows():
        scores = dot_lanes(queries[:, window] * own, keys[:, window]) * FACTOR
        if allowed is not None:
            scores = jnp.where(allowed, scores, -1e30)
        raised = jnp.exp(scores - jnp.max(scores, -1, keepdims=True))
        probs = raised * (1.0 / jnp.sum(raised, -1, keepdims=True))
        probs_ref[head] = probs
        attended[:, window] += dot(probs.astype(jnp.bfloat16), values[:, window] * own)


def score_grads(grad_attended, own, window, values, probs):
    grad_probs = dot_lanes(grad_attended[:, window] * own, values[:, window])
    totals = jnp.sum(probs * grad_probs, -1, keepdims=True)
    return (probs * (grad_probs - totals) * FACTOR).astype(jnp.bfloat16)


def from_blocks(blocks, wide):
    def step(pair, carry):
        rows = pl.ds(pl.multiple_of(8 * pair, 8), 8)
        wide[rows, :] = jnp.concatenate(
            [blocks[2 * pair].astype(jnp.float32), blocks[2 * pair + 1].astype(jnp.float32)], 0
        )
        return carry

    lax.fori_loop(0, MEMBERS // 2, step, 0)


def to_blocks(wide, blocks):
    def step(pair, carry):
        value = wide[pl.ds(pl.multiple_of(8 * pair, 8), 8), :]
        blocks[2 * pair] = value[:4].astype(jnp.bfloat16)
        blocks[2 * pair + 1] = value[4:].astype(jnp.bfloat16)
        return carry

    lax.fori_loop(0, MEMBERS // 2, step, 0)


def block_copy(away, source, target, sent, come, device):
    return pltpu.make_async_remote_copy(
        src_ref=source,
        dst_ref=target,
        send_sem=sent.at[away],
        recv_sem=come.at[away],
        device_id=device,
        device_id_type=MESH,
    )


def trade_start(leaving, coming, sent, come):
    outer, me = lax.axis_index("dp"), lax.axis_index("seq")

    def step(away, carry):
        there = lax.rem(me + away, MEMBERS)
        block_copy(
            away, leaving.at[there], coming.at[me], sent, come, (outer, there)
        ).start()
        return carry

    lax.fori_loop(1, MEMBERS, step, 0)
    coming[me] = leaving[me]


def trade_wait(leaving, coming, sent, come):
    outer, me = lax.axis_index("dp"), lax.axis_index("seq")

    def step(away, carry):
        there = lax.rem(me + away, MEMBERS)
        origin = lax.rem(me + MEMBERS - away, MEMBERS)
        block_copy(
            away, leaving.at[there], coming.at[origin], sent, come, (outer, there)
        ).wait()
        return carry

    lax.fori_loop(1, MEMBERS, step, 0)


def partners(place):
    outer = lax.axis_index("dp")
    me = lax.axis_index("seq")
    listed = [(outer, lax.rem(me + away, MEMBERS)) for away in range(1, MEMBERS)]
    listed += [place.z_to(step) for step in (1, -1, 2, -2)]
    slot = place.x * 2 + place.high
    for step in range(1, 8):
        there = lax.rem(slot + step, 8)
        listed.append(
            place.device(x=lax.div(there, 2), z=lax.rem(there, 2) * LOW + place.low)
        )
    return listed + [place.sibling()]


def advance(plans, rounds=1000):
    for _ in range(rounds):
        for plan in list(plans):
            if next(plan, plans) is plans:
                plans.remove(plan)
        if not plans:
            return


def split_packed(packed, rows, queries, keys, values):
    queries[...] = packed[:TOKENS, :INNER].astype(jnp.bfloat16)
    keys[...] = packed[:rows, INNER : 2 * INNER].astype(jnp.bfloat16)
    values[...] = packed[:rows, 2 * INNER : 3 * INNER].astype(jnp.bfloat16)


def scratch_table():
    f32, b16 = jnp.float32, jnp.bfloat16
    half = MERGE_TILES // 2
    project, merge = (MODEL, 3 * INNER), (INNER, MODEL)
    wide, narrow = (TOKENS, MODEL), (TOKENS, INNER)
    blocks = (MEMBERS, 4, MODEL)
    sems = pltpu.SemaphoreType.DMA
    return {
        "held": pltpu.VMEM((LOW, RING, HELD_TILES) + TILE, b16),
        "local": pltpu.VMEM((HELD_TILES,) + TILE, b16),
        "staged": pltpu.VMEM((4,) + TILE, f32),
        "loose": pltpu.VMEM((8, 1792), f32),
        "stage": pltpu.VMEM((144, 1792), f32),
        "space_project": pltpu.VMEM(project, b16),
        "space_merge": pltpu.VMEM(merge, b16),
        "time_project": pltpu.VMEM(project, b16),
        "time_merge": pltpu.VMEM(merge, b16),
        "gather_sent": sems((3, GATHER_COPIES)),
        "gather_come": sems((3, GATHER_COPIES)),
        "reduce_stage": pltpu.VMEM((144, MODEL), f32),
        "reduce_staged": pltpu.VMEM((RING, 3) + TILE, f32),
        "part": pltpu.VMEM(merge, f32),
        "packed_part": pltpu.VMEM((LOW, RING, MERGE_TILES) + TILE, b16),
        "near": pltpu.VMEM((LOW, RING, half) + TILE, b16),
        "total": pltpu.VMEM((LOW, RING, half) + TILE, b16),
        "z_in": pltpu.VMEM((3, RING, Z_TILES) + TILE, b16),
        "z_sum": pltpu.VMEM((RING, Z_TILES) + TILE, b16),
        "zy_in": pltpu.VMEM((RING - 1, Z_TILES) + TILE, b16),
        "y_in": pltpu.VMEM((RING - 1, LOW, half - Z_TILES) + TILE, b16),
        "y_sum": pltpu.VMEM((LOW, half - Z_TILES) + TILE, b16),
        "yz_in": pltpu.VMEM((3, half - Z_TILES) + TILE, b16),
        "parts": pltpu.VMEM((8, half) + TILE, b16),
        "final": pltpu.VMEM((MERGE_TILES,) + TILE, f32),
        "reduce_sent": sems((REDUCE_COPIES,)),
        "reduce_come": sems((REDUCE_COPIES,)),
        "both_tokens": pltpu.VMEM((2,) + wide, b16),
        "modulated": pltpu.VMEM((2 * TOKENS, MODEL), b16),
        "packed": pltpu.VMEM((2 * TOKENS, 1792), f32),
        "space_normed": pltpu.VMEM(wide, f32),
        "space_inverse": pltpu.VMEM((TOKENS, 1), f32),
        "space_queries": pltpu.VMEM(narrow, b16),
        "space_keys": pltpu.VMEM((2 * TOKENS, INNER), b16),
        "space_values": pltpu.VMEM((2 * TOKENS, INNER), b16),
        "space_probs": pltpu.VMEM((HEADS, TOKENS, 2 * TOKENS), f32),
        "attended": pltpu.VMEM(narrow, f32),
        "time_normed": pltpu.VMEM(wide, f32),
        "time_queries": pltpu.VMEM(narrow, b16),
        "time_keys": pltpu.VMEM(narrow, b16),
        "time_values": pltpu.VMEM(narrow, b16),
        "time_probs": pltpu.VMEM((HEADS, TOKENS, TOKENS), f32),
        "wide": pltpu.VMEM(wide, f32),
        "across": pltpu.VMEM(wide, f32),
        "grad_result": pltpu.VMEM(wide, f32),
        "grad_attended": pltpu.VMEM(narrow, b16),
        "grad_scores": pltpu.VMEM((HEADS, TOKENS, 2 * TOKENS), b16),
        "grad_queries": pltpu.VMEM(narrow, f32),
        "grad_keys": pltpu.VMEM((2 * TOKENS, INNER), f32),
        "grad_values": pltpu.VMEM((2 * TOKENS, INNER), f32),
        "grad_packed": pltpu.VMEM((TOKENS, 1792), f32),
        "far_out": pltpu.VMEM((2,) + narrow, b16),
        "far_in": pltpu.VMEM((2,) + narrow, b16),
        "middle_out": pltpu.VMEM(blocks, b16),
        "middle_in": pltpu.VMEM(blocks, b16),
        "grad_out": pltpu.VMEM(blocks, b16),
        "grad_in": pltpu.VMEM(blocks, b16),
        "middle_sent": sems((MEMBERS,)),
        "middle_come": sems((MEMBERS,)),
        "grad_sent": sems((MEMBERS,)),
        "grad_come": sems((MEMBERS,)),
        "pair_sent": sems((2,)),
        "pair_come": sems((2,)),
    }


class Refs:
    def __init__(self, refs):
        for name, ref in zip(scratch_table(), refs, strict=True):
            setattr(self, name, ref)


def join_packed(grad_packed, queries, keys, values):
    grad_packed[:, :INNER] = queries
    grad_packed[:, INNER : 2 * INNER] = keys
    grad_packed[:, 2 * INNER : 3 * INNER] = values
    return grad_packed[:, : 3 * INNER].astype(jnp.bfloat16)


def clip_kernel(
    tokens,
    modulation,
    space_project,
    space_merge,
    time_project,
    time_merge,
    cotangent,
    result,
    token_grads,
    merge_grads,
    *scratch,
):
    at = Refs(scratch)
    place = Place()
    expected = greet(partners(place))

    def row(index):
        return modulation[index : index + 1, :]

    starts = (0, PROJECT_TILES, PROJECT_TILES + MERGE_TILES, 2 * PROJECT_TILES + MERGE_TILES)
    for shard, start in zip((space_project, space_merge, time_project, time_merge), starts):
        pack_own(shard, at.staged, at.loose, at.local, start)
    at.both_tokens[0] = tokens[...]
    links = [Link(at.gather_sent.at[i], at.gather_come.at[i]) for i in range(3)]
    groups = [
        Gather(place, links[0], at.held, starts[0], 2, 3, 5),
        Gather(place, links[1], at.held, starts[1], 1, 1, 1),
        Gather(place, links[2], at.held, starts[2], 2, 6, 8),
    ]
    for group in groups:
        group.hold_own(at.local)
    plans = {name: [group.plan()] for name, group in zip("SMT", groups)}

    def steps(order):
        for name in order:
            advance(plans[name], 1)

    pl.semaphore_wait(pltpu.get_barrier_semaphore(), expected)
    steps("SMT")
    pair = Link(at.pair_sent, at.pair_come)
    partner = place.y_to(1 - 2 * lax.rem(place.y, 2))
    number = pair.send(at.both_tokens.at[0], at.both_tokens.at[1], partner)
    normed, inverse_std = normalize(tokens[...].astype(jnp.float32))
    at.space_normed[...] = normed
    at.space_inverse[...] = inverse_std
    at.modulated[:TOKENS] = (normed * (1.0 + row(1)) + row(0)).astype(jnp.bfloat16)
    from_blocks(cotangent, at.grad_result)
    steps("SM")
    pair.arrived(number, at.both_tokens.at[1], partner)
    normed, _ = normalize(at.both_tokens[1].astype(jnp.float32))
    at.modulated[TOKENS:] = (normed * (1.0 + row(1)) + row(0)).astype(jnp.bfloat16)
    steps("SMTSMSM")
    advance(plans["S"])
    unpack_all(at.held, starts[0], 36, 1728, at.stage, at.space_project)

    at.packed[:, : 3 * INNER] = dot(at.modulated[...], at.space_project[...])
    split_packed(at.packed, 2 * TOKENS, at.space_queries, at.space_keys, at.space_values)
    steps("T")
    attend(at.space_queries, at.space_keys, at.space_values, at.space_probs, at.attended)
    advance(plans["M"])
    unpack_all(at.held, starts[1], 18, 1152, at.stage, at.space_merge)
    branch = dot(at.attended[...].astype(jnp.bfloat16), at.space_merge[...])
    at.wide[...] = tokens[...].astype(jnp.float32) + row(2) * branch
    to_blocks(at.wide, at.middle_out)
    trade_start(at.middle_out, at.middle_in, at.middle_sent, at.middle_come)
    advance(plans["T"])
    unpack_all(at.held, starts[2], 36, 1728, at.stage, at.time_project)
    unpack_all(at.held, starts[3], 18, 1152, at.stage, at.time_merge)
    scaled = (row(5) * at.grad_result[...]).astype(jnp.bfloat16)
    at.grad_attended[...] = dot_lanes(scaled, at.time_merge[...]).astype(jnp.bfloat16)
    trade_wait(at.middle_out, at.middle_in, at.middle_sent, at.middle_come)
    from_blocks(at.middle_in, at.across)

    normed, time_inverse = normalize(at.across[...])
    at.time_normed[...] = normed
    modulated = (normed * (1.0 + row(4)) + row(3)).astype(jnp.bfloat16)
    at.packed[:TOKENS, : 3 * INNER] = dot(modulated, at.time_project[...])
    split_packed(at.packed, TOKENS, at.time_queries, at.time_keys, at.time_values)
    square = (TOKENS, TOKENS)
    patch_row = lax.rem(lax.broadcasted_iota(jnp.int32, square, 0), 8)
    patch_column = lax.rem(lax.broadcasted_iota(jnp.int32, square, 1), 8)
    attend(
        at.time_queries,
        at.time_keys,
        at.time_values,
        at.time_probs,
        at.attended,
        patch_row == patch_column,
    )
    flat = at.attended[...].astype(jnp.bfloat16)
    scaled = (row(5) * at.grad_result[...]).astype(jnp.bfloat16)
    at.part[...] = dot_rows(flat, scaled)
    pack_partial(at.part, at.reduce_stage, at.reduce_staged, at.packed_part)
    reducing = Link(at.reduce_sent, at.reduce_come)
    reduction = [
        reduce_plan(
            place, reducing, at.packed_part, at.near, at.total, at.z_in, at.z_sum, at.zy_in,
            at.y_in, at.y_sum, at.yz_in, at.parts, at.final,
        )
    ]
    advance(reduction, 1)
    at.wide[...] = at.across[...] + row(5) * dot(flat, at.time_merge[...])
    to_blocks(at.wide, result)
    advance(reduction, 1)

    at.grad_queries[...] = jnp.zeros_like(at.grad_queries)
    at.grad_keys[...] = jnp.zeros_like(at.grad_keys)
    at.grad_values[...] = jnp.zeros_like(at.grad_values)
    for head, window, own in head_windows():
        probs = at.time_probs[head]
        grads = score_grads(at.grad_attended, own, window, at.time_values, probs)
        at.grad_values[:TOKENS, window] += dot_rows(
            probs.astype(jnp.bfloat16), at.grad_attended[:, window] * own
        )
        at.grad_keys[:TOKENS, window] += dot_rows(grads, at.time_queries[:, window] * own)
        at.grad_queries[:, window] += dot(grads, at.time_keys[:, window] * own)
    grad_packed = join_packed(
        at.grad_packed, at.grad_queries[...], at.grad_keys[:TOKENS], at.grad_values[:TOKENS]
    )
    grad_modulated = dot_lanes(grad_packed, at.time_project[...])
    at.wide[...] = at.grad_result[...] + modulate_back(
        grad_modulated, at.time_normed[...], time_inverse, row(4)
    )
    to_blocks(at.wide, at.grad_out)
    trade_start(at.grad_out, at.grad_in, at.grad_sent, at.grad_come)
    advance(reduction, 2)
    trade_wait(at.grad_out, at.grad_in, at.grad_sent, at.grad_come)
    from_blocks(at.grad_in, at.wide)

    scaled = (row(2) * at.wide[...]).astype(jnp.bfloat16)
    at.grad_attended[...] = dot_lanes(scaled, at.space_merge[...]).astype(jnp.bfloat16)
    at.grad_keys[...] = jnp.zeros_like(at.grad_keys)
    at.grad_values[...] = jnp.zeros_like(at.grad_values)
    at.grad_queries[...] = jnp.zeros_like(at.grad_queries)
    far = pl.ds(TOKENS, TOKENS)
    for head, window, own in head_windows():
        probs = at.space_probs[head]
        grads = score_grads(at.grad_attended, own, window, at.space_values, probs)
        at.grad_scores[head] = grads
        at.grad_values[:, window] += dot_rows(
            probs.astype(jnp.bfloat16), at.grad_attended[:, window] * own
        )
        at.grad_keys[:, window] += dot_rows(grads, at.space_queries[:, window] * own)
    at.far_out[0] = at.grad_keys[far, :].astype(jnp.bfloat16)
    at.far_out[1] = at.grad_values[far, :].astype(jnp.bfloat16)
    number = pair.send(at.far_out, at.far_in, partner)
    advance(reduction, 1)
    for head, window, own in head_windows():
        at.grad_queries[:, window] += dot(at.grad_scores[head], at.space_keys[:, window] * own)
    advance(reduction, 1)
    pair.arrived(number, at.far_in, partner)
    grad_packed = join_packed(
        at.grad_packed,
        at.grad_queries[...],
        at.grad_keys[:TOKENS] + at.far_in[0].astype(jnp.float32),
        at.grad_values[:TOKENS] + at.far_in[1].astype(jnp.float32),
    )
    advance(reduction, 1)
    grad_modulated = dot_lanes(grad_packed, at.space_project[...])
    token_grads[...] = (
        at.wide[...]
        + modulate_back(grad_modulated, at.space_normed[...], at.space_inverse[...], row(1))
    ).astype(jnp.bfloat16)
    advance(reduction)
    unpack_final(at.final, merge_grads)
    for link in links + [pair, reducing]:
        link.finish()


def body(
    tokens, modulation, spatial_project, spatial_merge, temporal_project, temporal_merge, cotangent
):
    vmem = pl.BlockSpec(memory_space=pltpu.VMEM)
    blocks = (MEMBERS, 4, MODEL)
    result, token_grads, merge_grads = pl.pallas_call(
        clip_kernel,
        out_shape=[
            jax.ShapeDtypeStruct(blocks, jnp.bfloat16),
            jax.ShapeDtypeStruct((TOKENS, MODEL), jnp.bfloat16),
            jax.ShapeDtypeStruct((18, MODEL), jnp.float32),
        ],
        in_specs=[vmem] * 7,
        out_specs=[vmem] * 3,
        scratch_shapes=list(scratch_table().values()),
        compiler_params=pltpu.CompilerParams(
            collective_id=0, has_side_effects=True, vmem_limit_bytes=60 * 1024 * 1024
        ),
        cost_estimate=pl.CostEstimate(
            flops=3_000_000_000, bytes_accessed=4_000_000, transcendentals=500_000
        ),
        name="clip_step",
    )(
        tokens.reshape(TOKENS, MODEL),
        modulation.reshape(6, MODEL),
        spatial_project,
        spatial_merge,
        temporal_project,
        temporal_merge,
        cotangent.reshape(blocks),
    )
    return (
        result.reshape(1, 16, 2, 4, MODEL),
        token_grads.reshape(1, 1, TOKENS, MODEL),
        merge_grads,
    )


def solution(mesh):
    in_specs = (
        P("dp", "seq", None, None),
        P("dp", None, None),
        P("seq", None),
        P("seq", None),
        P("seq", None),
        P("seq", None),
        P("dp", None, None, "seq", None),
    )
    out_specs = (P("dp", None, None, "seq", None), P("dp", "seq", None, None), P("seq", None))
    return jax.shard_map(body, mesh=mesh, in_specs=in_specs, out_specs=out_specs, check_vma=False)
```

```python
import jax
import jax.numpy as jnp
from jax import lax
from jax.experimental import pallas as pl
from jax.experimental.pallas import tpu as pltpu
from jax.sharding import PartitionSpec as P

HEAD_DIM = 72
MESH = pl.DeviceIdType.MESH
LOW, RING = 4, 8
TILE = (16, 128)


class Place:
    def __init__(self):
        outer = lax.axis_index("dp")
        inner = lax.axis_index("seq")
        self.core = lax.rem(outer, 2)
        self.high = lax.rem(lax.div(outer, 2), 2)
        self.x = lax.div(outer, 4)
        self.low = lax.div(inner, RING)
        self.y = lax.rem(inner, RING)
        self.z = self.high * LOW + self.low
        self.way = 1 - 2 * self.core

    def low_at(self, step):
        return lax.rem(self.low + step + LOW, LOW)

    def y_at(self, step):
        return lax.rem(self.y + step + RING, RING)

    def device(self, x=None, y=None, z=None, core=None):
        x = self.x if x is None else x
        y = self.y if y is None else y
        z = self.z if z is None else z
        core = self.core if core is None else core
        outer = (x * 2 + lax.div(z, LOW)) * 2 + core
        return (outer, lax.rem(z, LOW) * RING + y)

    def y_to(self, step):
        return self.device(y=self.y_at(step))

    def x_at(self, step):
        return lax.rem(self.x + step + 4, 4)

    def x_to(self, step):
        return self.device(x=self.x_at(step))

    def z_to(self, step):
        return self.device(z=lax.rem(self.z + step + RING, RING))

    def sibling(self):
        return self.device(core=1 - self.core)


def greet(devices):
    barrier = pltpu.get_barrier_semaphore()
    for device in devices:
        pl.semaphore_signal(barrier, inc=1, device_id=device, device_id_type=MESH)
    return len(devices)


class Link:
    def __init__(self, send_sems, recv_sems):
        self.send_sems, self.recv_sems = send_sems, recv_sems
        self.count = 0
        self.started = []

    def number(self):
        self.count += 1
        return self.count - 1

    def copy(self, number, source, target, device):
        return pltpu.make_async_remote_copy(
            src_ref=source,
            dst_ref=target,
            send_sem=self.send_sems.at[number],
            recv_sem=self.recv_sems.at[number],
            device_id=device,
            device_id_type=MESH,
        )

    def send(self, source, target, device):
        number = self.number()
        copy = self.copy(number, source, target, device)
        copy.start()
        self.started.append(copy)
        return number

    def arrived(self, number, target, device):
        self.copy(number, target, target, device).wait_recv()

    def finish(self):
        for copy in self.started:
            copy.wait_send()
        self.started = []


class Gather:
    def __init__(self, place, link, held, begin, sliced, y_count, z_count):
        self.place, self.link, self.held = place, link, held
        self.begin, self.sliced = begin, sliced
        self.rest = begin + 8 * sliced
        self.y_count, self.z_count = y_count, z_count
        self.size = 8 * sliced + 2 * (y_count + z_count)

    def slice_of(self, x, core):
        return pl.ds(self.begin + (x * 2 + core) * self.sliced, self.sliced)

    def y_part(self, core):
        return pl.ds(self.rest + core * (self.y_count + self.z_count), self.y_count)

    def z_part(self, core):
        return pl.ds(
            self.rest + core * (self.y_count + self.z_count) + self.y_count, self.z_count
        )

    def hold_own(self, local):
        place, held = self.place, self.held
        for count, tiles in (
            (self.sliced, self.slice_of(place.x, place.core)),
            (self.y_count, self.y_part(place.core)),
            (self.z_count, self.z_part(place.core)),
        ):
            if count:
                held[place.low, place.y, tiles] = local[tiles]

    def go(self, ref, device):
        return self.link.send(ref, ref, device)

    def across_y(self, tiles):
        place = self.place
        return [
            (self.go(self.held.at[place.low, place.y, tiles], place.y_to(step)), step)
            for step in range(1, RING)
        ]

    def arrived_y(self, numbers, tiles):
        place = self.place
        for number, step in numbers:
            self.link.arrived(
                number, self.held.at[place.low, place.y_at(-step), tiles], place.y_to(step)
            )

    def across_z(self, part):
        place = self.place
        return [
            (self.go(part(0), place.z_to(1)), -1),
            (self.go(part(0), place.z_to(-1)), 1),
            (self.go(part(0), place.z_to(2 * place.way)), 2),
        ]

    def arrived_z(self, numbers, part):
        for number, step in numbers:
            self.link.arrived(number, part(step), self.place.z_to(1))

    def share(self, refs):
        return [self.go(ref, self.place.sibling()) for ref in refs]

    def shared(self, numbers, refs):
        for number, ref in zip(numbers, refs, strict=True):
            self.link.arrived(number, ref, self.place.sibling())

    def over_x(self):
        place, held = self.place, self.held
        mine = self.slice_of(place.x, place.core)

        def ring(step):
            return held.at[place.low_at(step), :, mine]

        def whole(step, core):
            return held.at[:, :, self.slice_of(place.x_at(step), core)]

        numbers = self.across_y(mine)
        yield
        self.arrived_y(numbers, mine)
        numbers = self.across_z(ring)
        yield
        self.arrived_z(numbers, ring)
        block = whole(0, place.core)
        plus, minus = self.go(block, place.x_to(1)), self.go(block, place.x_to(-1))
        given = self.share([block])
        yield
        self.link.arrived(plus, whole(-1, place.core), place.x_to(1))
        self.link.arrived(minus, whole(1, place.core), place.x_to(-1))
        last = self.go(whole(-place.way, place.core), place.x_to(place.way))
        given += self.share([whole(-1, place.core), whole(1, place.core)])
        yield
        self.link.arrived(last, whole(2, place.core), place.x_to(1))
        given += self.share([whole(2, place.core)])
        yield
        self.shared(given, [whole(step, 1 - place.core) for step in (0, -1, 1, 2)])
        yield

    def y_first(self):
        place, held = self.place, self.held
        mine, other = self.y_part(place.core), self.y_part(1 - place.core)

        def ring(step):
            return held.at[place.low_at(step), :, mine]

        numbers = self.across_y(mine)
        yield
        self.arrived_y(numbers, mine)
        numbers = self.across_z(ring)
        given = self.share([ring(0)])
        yield
        self.arrived_z(numbers, ring)
        given += self.share([ring(step) for step in (-1, 1, 2)])
        yield
        self.shared(given, [held.at[place.low_at(step), :, other] for step in (0, -1, 1, 2)])
        yield

    def z_first(self):
        place, held = self.place, self.held
        mine, other = self.z_part(place.core), self.z_part(1 - place.core)

        def one(step):
            return held.at[place.low_at(step), place.y, mine]

        def run(step):
            return held.at[:, place.y_at(step), mine]

        numbers = self.across_z(one)
        yield
        self.arrived_z(numbers, one)
        near = (1, -1, 2, -2)
        numbers = [self.go(run(0), place.y_to(step)) for step in near]
        given = self.share([run(0)])
        yield
        for number, step in zip(numbers, near, strict=True):
            self.link.arrived(number, run(-step), place.y_to(step))
        numbers = [
            self.go(run(-2), place.y_to(1)),
            self.go(run(2), place.y_to(-1)),
            self.go(run(-2 * place.way), place.y_to(2 * place.way)),
        ]
        given += self.share([run(-step) for step in near])
        yield
        far = (-3, 3, 4)
        for number, step in zip(numbers, far, strict=True):
            self.link.arrived(number, run(step), place.y_to(1))
        given += self.share([run(step) for step in far])
        yield
        steps = (0,) + tuple(-step for step in near) + far
        self.shared(given, [held.at[:, place.y_at(step), other] for step in steps])
        yield

    def plan(self):
        plans = [self.over_x()] if self.sliced else []
        plans += [self.z_first()] if self.z_count else []
        plans += [self.y_first()] if self.y_count else []
        while plans:
            for plan in list(plans):
                if next(plan, plans) is plans:
                    plans.remove(plan)
            yield


def lane_tiles(width):
    return [(at, min(128, width - at)) for at in range(0, width, 128)]


def pack_own(shard, staged, wide, local, begin):
    rows, width = shard.shape
    full, rest = rows // 16, rows % 16
    tiles = lane_tiles(width)
    number = begin
    for block in range(full):
        for at, lanes in tiles:
            local[number, :, :lanes] = shard[16 * block : 16 * block + 16, at : at + lanes]
            number += 1
    per = 16 // rest
    wide[:rest, :width] = shard[16 * full :, :].astype(jnp.float32)
    groups = -(-len(tiles) // per)
    for index, (at, lanes) in enumerate(tiles):
        staged[index // per, pl.ds(rest * (index % per), rest), :lanes] = wide[
            :rest, at : at + lanes
        ]
    for group in range(groups):
        local[number + group] = staged[group].astype(jnp.bfloat16)


def unpack_all(held, begin, rows, width, stage, out):
    full, rest = rows // 16, rows % 16
    tiles = lane_tiles(width)
    per = 16 // rest
    several = 4 if rows == 36 else 8
    block = several * rows

    def step(index, carry):
        low, y = lax.div(index * several, RING), lax.rem(index * several, RING)
        for shard in range(several):
            top = shard * rows
            for part in range(full):
                for tile, (at, lanes) in enumerate(tiles):
                    value = held[low, y + shard, begin + part * len(tiles) + tile]
                    stage[top + 16 * part : top + 16 * part + 16, at : at + lanes] = value.astype(
                        jnp.float32
                    )[:, :lanes]
            for group in range(-(-len(tiles) // per)):
                value = held[low, y + shard, begin + full * len(tiles) + group]
                value = value.astype(jnp.float32)
                for piece in range(per):
                    tile = group * per + piece
                    if tile < len(tiles):
                        at, lanes = tiles[tile]
                        stage[top + 16 * full : top + rows, at : at + lanes] = value[
                            rest * piece : rest * piece + rest, :lanes
                        ]
        out[pl.ds(pl.multiple_of(index * block, 16), block), :] = stage[:block, :width].astype(
            jnp.bfloat16
        )
        return carry

    lax.fori_loop(0, 32 // several, step, 0)


PROJECT_TILES, MERGE_TILES = 32, 12
HELD_TILES = 2 * (PROJECT_TILES + MERGE_TILES)
GATHER_COPIES = 52
REDUCE_COPIES = 32


Z_TILES = 4


def reduce_plan(place, link, packed, near, total, z_in, z_sum, zy_in, y_in, y_sum, yz_in, parts, final):
    half = MERGE_TILES // 2
    mine, other = place.core * half, (1 - place.core) * half
    sibling = place.sibling()
    first, second = pl.ds(0, Z_TILES), pl.ds(Z_TILES, half - Z_TILES)
    f32, b16 = jnp.float32, jnp.bfloat16
    lows = ((1, 1), (-1, -1), (2, 2 * place.way))
    number = link.send(packed.at[:, :, pl.ds(other, half)], near, sibling)
    yield
    link.arrived(number, near, sibling)

    def add(low, carry):
        for y in range(RING):
            total[low, y] = (
                packed[low, y, pl.ds(mine, half)].astype(f32) + near[low, y].astype(f32)
            ).astype(b16)
        return carry

    lax.fori_loop(0, LOW, add, 0)
    z_numbers = [
        link.send(total.at[place.low_at(step), :, first], z_in.at[slot], place.z_to(hops))
        for slot, (step, hops) in enumerate(lows)
    ]
    y_numbers = [
        link.send(total.at[:, place.y_at(step), second], y_in.at[step - 1], place.y_to(step))
        for step in range(1, RING)
    ]
    yield
    value = total[place.low, :, first].astype(f32)
    for slot, number in enumerate(z_numbers):
        link.arrived(number, z_in.at[slot], sibling)
        value = value + z_in[slot].astype(f32)
    z_sum[...] = value.astype(b16)
    z_numbers = [
        link.send(z_sum.at[place.y_at(step)], zy_in.at[step - 1], place.y_to(step))
        for step in range(1, RING)
    ]
    value = total[:, place.y, second].astype(f32)
    for slot, number in enumerate(y_numbers):
        link.arrived(number, y_in.at[slot], sibling)
        value = value + y_in[slot].astype(f32)
    y_sum[...] = value.astype(b16)
    y_numbers = [
        link.send(y_sum.at[place.low_at(step)], yz_in.at[slot], place.z_to(hops))
        for slot, (step, hops) in enumerate(lows)
    ]
    yield
    value = z_sum[place.y].astype(f32)
    for slot, number in enumerate(z_numbers):
        link.arrived(number, zy_in.at[slot], sibling)
        value = value + zy_in[slot].astype(f32)
    me = place.x * 2 + place.high
    parts[me, first] = value.astype(b16)
    value = y_sum[place.low].astype(f32)
    for slot, number in enumerate(y_numbers):
        link.arrived(number, yz_in.at[slot], sibling)
        value = value + yz_in[slot].astype(f32)
    parts[me, second] = value.astype(b16)
    numbers = []
    for step in range(1, 8):
        there = lax.rem(me + step, 8)
        device = place.device(
            x=lax.div(there, 2), z=lax.rem(there, 2) * LOW + place.low
        )
        numbers.append(link.send(parts.at[me], parts.at[me], device))
    yield
    for step, number in enumerate(numbers, 1):
        link.arrived(number, parts.at[lax.rem(me - step + 8, 8)], sibling)
    value = parts[0].astype(f32)
    for index in range(1, 8):
        value = value + parts[index].astype(f32)
    final[pl.ds(mine, half)] = value
    number = link.send(final.at[pl.ds(mine, half)], final.at[pl.ds(mine, half)], sibling)
    yield
    link.arrived(number, final.at[pl.ds(other, half)], sibling)


def pack_partial(part, stage, staged, packed):
    def step(low, carry):
        stage[...] = part[pl.ds(pl.multiple_of(low * 144, 16), 144), :].astype(jnp.float32)
        staged[...] = jnp.zeros_like(staged)
        for y in range(RING):
            for tile in range(9):
                at = 128 * tile
                packed[low, y, tile] = stage[18 * y : 18 * y + 16, at : at + 128].astype(
                    jnp.bfloat16
                )
                staged[y, tile // 8, 2 * (tile % 8) : 2 * (tile % 8) + 2, :] = stage[
                    18 * y + 16 : 18 * y + 18, at : at + 128
                ]
            for group in range(3):
                packed[low, y, 9 + group] = staged[y, group].astype(jnp.bfloat16)
        return carry

    lax.fori_loop(0, LOW, step, 0)


def unpack_final(final, out):
    for tile in range(9):
        at = 128 * tile
        out[0:16, at : at + 128] = final[tile]
        out[16:18, at : at + 128] = final[9 + tile // 8, 2 * (tile % 8) : 2 * (tile % 8) + 2, :]


MEMBERS, TOKENS, MODEL, INNER, HEADS = 32, 128, 1152, 576, 8
EPSILON = 1e-06
FACTOR = HEAD_DIM ** (-0.5)


def dot(left, right):
    return jnp.dot(left, right, preferred_element_type=jnp.float32)


def dot_lanes(left, right):
    return lax.dot_general(left, right, (((1,), (1,)), ((), ())), preferred_element_type=jnp.float32)


def dot_rows(left, right):
    return lax.dot_general(left, right, (((0,), (0,)), ((), ())), preferred_element_type=jnp.float32)


def normalize(widened):
    average = jnp.mean(widened, -1, keepdims=True)
    centered = widened - average
    variance = jnp.mean(centered * centered, -1, keepdims=True)
    inverse_std = lax.rsqrt(variance + EPSILON)
    return (centered * inverse_std, inverse_std)


def modulate_back(grad_modulated, normed, inverse_std, scale_row):
    grad_normed = grad_modulated * (1.0 + scale_row)
    first_mean = jnp.mean(grad_normed, -1, keepdims=True)
    second_mean = jnp.mean(grad_normed * normed, -1, keepdims=True)
    return inverse_std * (grad_normed - first_mean - normed * second_mean)


def head_windows():
    for head in range(HEADS):
        first = HEAD_DIM * head
        start, stop = first // 128 * 128, min(INNER, -(-(first + HEAD_DIM) // 128) * 128)
        lane = lax.broadcasted_iota(jnp.int32, (1, stop - start), 1) + start
        inside = jnp.logical_and(lane >= first, lane < first + HEAD_DIM)
        yield head, slice(start, stop), jnp.where(inside, 1.0, 0.0).astype(jnp.bfloat16)


def attend(queries, keys, values, probs_ref, attended, allowed=None):
    attended[...] = jnp.zeros_like(attended)
    for head, window, own in head_windows():
        scores = dot_lanes(queries[:, window] * own, keys[:, window]) * FACTOR
        if allowed is not None:
            scores = jnp.where(allowed, scores, -1e30)
        raised = jnp.exp(scores - jnp.max(scores, -1, keepdims=True))
        probs = raised * (1.0 / jnp.sum(raised, -1, keepdims=True))
        probs_ref[head] = probs
        attended[:, window] += dot(probs[:TOKENS].astype(jnp.bfloat16), values[:, window] * own)


def score_grads(grad_attended, own, window, values, probs):
    grad_probs = dot_lanes(grad_attended[:, window] * own, values[:, window])
    totals = jnp.sum(probs * grad_probs, -1, keepdims=True)
    return (probs * (grad_probs - totals) * FACTOR).astype(jnp.bfloat16)


def from_blocks(blocks, wide):
    def step(pair, carry):
        rows = pl.ds(pl.multiple_of(8 * pair, 8), 8)
        wide[rows, :] = jnp.concatenate(
            [blocks[2 * pair].astype(jnp.float32), blocks[2 * pair + 1].astype(jnp.float32)], 0
        )
        return carry

    lax.fori_loop(0, MEMBERS // 2, step, 0)


def to_blocks(wide, blocks):
    def step(pair, carry):
        value = wide[pl.ds(pl.multiple_of(8 * pair, 8), 8), :]
        blocks[2 * pair] = value[:4].astype(jnp.bfloat16)
        blocks[2 * pair + 1] = value[4:].astype(jnp.bfloat16)
        return carry

    lax.fori_loop(0, MEMBERS // 2, step, 0)


def block_copy(away, source, target, sent, come, device):
    return pltpu.make_async_remote_copy(
        src_ref=source,
        dst_ref=target,
        send_sem=sent.at[away],
        recv_sem=come.at[away],
        device_id=device,
        device_id_type=MESH,
    )


def trade_start(leaving, coming, sent, come):
    outer, me = lax.axis_index("dp"), lax.axis_index("seq")

    def step(away, carry):
        there = lax.rem(me + away, MEMBERS)
        block_copy(
            away, leaving.at[there], coming.at[me], sent, come, (outer, there)
        ).start()
        return carry

    lax.fori_loop(1, MEMBERS, step, 0)
    coming[me] = leaving[me]


def trade_wait(leaving, coming, sent, come):
    outer, me = lax.axis_index("dp"), lax.axis_index("seq")

    def step(away, carry):
        there = lax.rem(me + away, MEMBERS)
        origin = lax.rem(me + MEMBERS - away, MEMBERS)
        block_copy(
            away, leaving.at[there], coming.at[origin], sent, come, (outer, there)
        ).wait()
        return carry

    lax.fori_loop(1, MEMBERS, step, 0)


def partners(place):
    outer = lax.axis_index("dp")
    me = lax.axis_index("seq")
    listed = [(outer, lax.rem(me + away, MEMBERS)) for away in range(1, MEMBERS)]
    listed += [place.z_to(step) for step in (1, -1, 2, -2)]
    slot = place.x * 2 + place.high
    for step in range(1, 8):
        there = lax.rem(slot + step, 8)
        listed.append(
            place.device(x=lax.div(there, 2), z=lax.rem(there, 2) * LOW + place.low)
        )
    return listed + [place.sibling()]


def advance(plans, rounds=1000):
    for _ in range(rounds):
        for plan in list(plans):
            if next(plan, plans) is plans:
                plans.remove(plan)
        if not plans:
            return


def split_packed(packed, rows, queries, keys, values):
    queries[...] = packed[:rows, :INNER].astype(jnp.bfloat16)
    keys[...] = packed[:rows, INNER : 2 * INNER].astype(jnp.bfloat16)
    values[...] = packed[:rows, 2 * INNER : 3 * INNER].astype(jnp.bfloat16)


def scratch_table():
    f32, b16 = jnp.float32, jnp.bfloat16
    half = MERGE_TILES // 2
    project, merge = (MODEL, 3 * INNER), (INNER, MODEL)
    wide, narrow = (TOKENS, MODEL), (TOKENS, INNER)
    blocks = (MEMBERS, 4, MODEL)
    sems = pltpu.SemaphoreType.DMA
    return {
        "held": pltpu.VMEM((LOW, RING, HELD_TILES) + TILE, b16),
        "local": pltpu.VMEM((HELD_TILES,) + TILE, b16),
        "staged": pltpu.VMEM((4,) + TILE, f32),
        "loose": pltpu.VMEM((8, 1792), f32),
        "stage": pltpu.VMEM((144, 1792), f32),
        "space_project": pltpu.VMEM(project, b16),
        "space_merge": pltpu.VMEM(merge, b16),
        "time_project": pltpu.VMEM(project, b16),
        "time_merge": pltpu.VMEM(merge, b16),
        "gather_sent": sems((3, GATHER_COPIES)),
        "gather_come": sems((3, GATHER_COPIES)),
        "reduce_stage": pltpu.VMEM((144, MODEL), f32),
        "reduce_staged": pltpu.VMEM((RING, 3) + TILE, f32),
        "part": pltpu.VMEM(merge, f32),
        "packed_part": pltpu.VMEM((LOW, RING, MERGE_TILES) + TILE, b16),
        "near": pltpu.VMEM((LOW, RING, half) + TILE, b16),
        "total": pltpu.VMEM((LOW, RING, half) + TILE, b16),
        "z_in": pltpu.VMEM((3, RING, Z_TILES) + TILE, b16),
        "z_sum": pltpu.VMEM((RING, Z_TILES) + TILE, b16),
        "zy_in": pltpu.VMEM((RING - 1, Z_TILES) + TILE, b16),
        "y_in": pltpu.VMEM((RING - 1, LOW, half - Z_TILES) + TILE, b16),
        "y_sum": pltpu.VMEM((LOW, half - Z_TILES) + TILE, b16),
        "yz_in": pltpu.VMEM((3, half - Z_TILES) + TILE, b16),
        "parts": pltpu.VMEM((8, half) + TILE, b16),
        "final": pltpu.VMEM((MERGE_TILES,) + TILE, f32),
        "reduce_sent": sems((REDUCE_COPIES,)),
        "reduce_come": sems((REDUCE_COPIES,)),
        "both_tokens": pltpu.VMEM((2,) + wide, b16),
        "modulated": pltpu.VMEM((2 * TOKENS, MODEL), b16),
        "packed": pltpu.VMEM((2 * TOKENS, 1792), f32),
        "space_normed": pltpu.VMEM(wide, f32),
        "space_inverse": pltpu.VMEM((TOKENS, 1), f32),
        "space_queries": pltpu.VMEM((2 * TOKENS, INNER), b16),
        "space_keys": pltpu.VMEM((2 * TOKENS, INNER), b16),
        "space_values": pltpu.VMEM((2 * TOKENS, INNER), b16),
        "space_probs": pltpu.VMEM((HEADS, 2 * TOKENS, 2 * TOKENS), f32),
        "attended": pltpu.VMEM(narrow, f32),
        "time_normed": pltpu.VMEM(wide, f32),
        "time_queries": pltpu.VMEM(narrow, b16),
        "time_keys": pltpu.VMEM(narrow, b16),
        "time_values": pltpu.VMEM(narrow, b16),
        "time_probs": pltpu.VMEM((HEADS, TOKENS, TOKENS), f32),
        "wide": pltpu.VMEM(wide, f32),
        "across": pltpu.VMEM(wide, f32),
        "grad_result": pltpu.VMEM(wide, f32),
        "grad_attended": pltpu.VMEM(narrow, b16),
        "grad_queries": pltpu.VMEM(narrow, f32),
        "grad_keys": pltpu.VMEM(narrow, f32),
        "grad_values": pltpu.VMEM(narrow, f32),
        "grad_packed": pltpu.VMEM((TOKENS, 1792), f32),
        "far_attended": pltpu.VMEM(narrow, b16),
        "near_attended": pltpu.VMEM(narrow, b16),
        "middle_out": pltpu.VMEM(blocks, b16),
        "middle_in": pltpu.VMEM(blocks, b16),
        "grad_out": pltpu.VMEM(blocks, b16),
        "grad_in": pltpu.VMEM(blocks, b16),
        "middle_sent": sems((MEMBERS,)),
        "middle_come": sems((MEMBERS,)),
        "grad_sent": sems((MEMBERS,)),
        "grad_come": sems((MEMBERS,)),
        "pair_sent": sems((2,)),
        "pair_come": sems((2,)),
    }


class Refs:
    def __init__(self, refs):
        for name, ref in zip(scratch_table(), refs, strict=True):
            setattr(self, name, ref)


def join_packed(grad_packed, queries, keys, values):
    grad_packed[:, :INNER] = queries
    grad_packed[:, INNER : 2 * INNER] = keys
    grad_packed[:, 2 * INNER : 3 * INNER] = values
    return grad_packed[:, : 3 * INNER].astype(jnp.bfloat16)


def clip_kernel(
    tokens,
    modulation,
    space_project,
    space_merge,
    time_project,
    time_merge,
    cotangent,
    result,
    token_grads,
    merge_grads,
    *scratch,
):
    at = Refs(scratch)
    place = Place()
    expected = greet(partners(place))

    def row(index):
        return modulation[0, index : index + 1, :]

    starts = (0, PROJECT_TILES, PROJECT_TILES + MERGE_TILES, 2 * PROJECT_TILES + MERGE_TILES)
    for shard, start in zip((space_project, space_merge, time_project, time_merge), starts):
        pack_own(shard, at.staged, at.loose, at.local, start)
    at.both_tokens[0] = tokens[...]
    links = [Link(at.gather_sent.at[i], at.gather_come.at[i]) for i in range(3)]
    groups = [
        Gather(place, links[0], at.held, starts[0], 2, 3, 5),
        Gather(place, links[1], at.held, starts[1], 1, 1, 1),
        Gather(place, links[2], at.held, starts[2], 2, 6, 8),
    ]
    for group in groups:
        group.hold_own(at.local)
    plans = {name: [group.plan()] for name, group in zip("SMT", groups)}

    def steps(order):
        for name in order:
            advance(plans[name], 1)

    pl.semaphore_wait(pltpu.get_barrier_semaphore(), expected)
    steps("SMT")
    pair = Link(at.pair_sent, at.pair_come)
    partner = place.y_to(1 - 2 * lax.rem(place.y, 2))
    number = pair.send(at.both_tokens.at[0], at.both_tokens.at[1], partner)
    normed, inverse_std = normalize(tokens[...].astype(jnp.float32))
    at.space_normed[...] = normed
    at.space_inverse[...] = inverse_std
    at.modulated[:TOKENS] = (normed * (1.0 + row(1)) + row(0)).astype(jnp.bfloat16)
    from_blocks(cotangent, at.grad_result)
    steps("SM")
    pair.arrived(number, at.both_tokens.at[1], partner)
    normed, _ = normalize(at.both_tokens[1].astype(jnp.float32))
    at.modulated[TOKENS:] = (normed * (1.0 + row(1)) + row(0)).astype(jnp.bfloat16)
    steps("SMTSMSM")
    advance(plans["S"])
    unpack_all(at.held, starts[0], 36, 1728, at.stage, at.space_project)

    at.packed[:, : 3 * INNER] = dot(at.modulated[...], at.space_project[...])
    split_packed(at.packed, 2 * TOKENS, at.space_queries, at.space_keys, at.space_values)
    steps("T")
    attend(at.space_queries, at.space_keys, at.space_values, at.space_probs, at.attended)
    advance(plans["M"])
    unpack_all(at.held, starts[1], 18, 1152, at.stage, at.space_merge)
    branch = dot(at.attended[...].astype(jnp.bfloat16), at.space_merge[...])
    at.wide[...] = tokens[...].astype(jnp.float32) + row(2) * branch
    to_blocks(at.wide, at.middle_out)
    trade_start(at.middle_out, at.middle_in, at.middle_sent, at.middle_come)
    advance(plans["T"])
    unpack_all(at.held, starts[2], 36, 1728, at.stage, at.time_project)
    unpack_all(at.held, starts[3], 18, 1152, at.stage, at.time_merge)
    scaled = (row(5) * at.grad_result[...]).astype(jnp.bfloat16)
    at.grad_attended[...] = dot_lanes(scaled, at.time_merge[...]).astype(jnp.bfloat16)
    trade_wait(at.middle_out, at.middle_in, at.middle_sent, at.middle_come)
    from_blocks(at.middle_in, at.across)

    normed, time_inverse = normalize(at.across[...])
    at.time_normed[...] = normed
    modulated = (normed * (1.0 + row(4)) + row(3)).astype(jnp.bfloat16)
    at.packed[:TOKENS, : 3 * INNER] = dot(modulated, at.time_project[...])
    split_packed(at.packed, TOKENS, at.time_queries, at.time_keys, at.time_values)
    square = (TOKENS, TOKENS)
    patch_row = lax.rem(lax.broadcasted_iota(jnp.int32, square, 0), 8)
    patch_column = lax.rem(lax.broadcasted_iota(jnp.int32, square, 1), 8)
    attend(
        at.time_queries,
        at.time_keys,
        at.time_values,
        at.time_probs,
        at.attended,
        patch_row == patch_column,
    )
    flat = at.attended[...].astype(jnp.bfloat16)
    scaled = (row(5) * at.grad_result[...]).astype(jnp.bfloat16)
    at.part[...] = dot_rows(flat, scaled)
    pack_partial(at.part, at.reduce_stage, at.reduce_staged, at.packed_part)
    reducing = Link(at.reduce_sent, at.reduce_come)
    reduction = [
        reduce_plan(
            place, reducing, at.packed_part, at.near, at.total, at.z_in, at.z_sum, at.zy_in,
            at.y_in, at.y_sum, at.yz_in, at.parts, at.final,
        )
    ]
    advance(reduction, 1)
    at.wide[...] = at.across[...] + row(5) * dot(flat, at.time_merge[...])
    to_blocks(at.wide, result)
    advance(reduction, 1)

    at.grad_queries[...] = jnp.zeros_like(at.grad_queries)
    at.grad_keys[...] = jnp.zeros_like(at.grad_keys)
    at.grad_values[...] = jnp.zeros_like(at.grad_values)
    for head, window, own in head_windows():
        probs = at.time_probs[head]
        grads = score_grads(at.grad_attended, own, window, at.time_values, probs)
        at.grad_values[:, window] += dot_rows(
            probs.astype(jnp.bfloat16), at.grad_attended[:, window] * own
        )
        at.grad_keys[:, window] += dot_rows(grads, at.time_queries[:, window] * own)
        at.grad_queries[:, window] += dot(grads, at.time_keys[:, window] * own)
    grad_packed = join_packed(
        at.grad_packed, at.grad_queries[...], at.grad_keys[...], at.grad_values[...]
    )
    grad_modulated = dot_lanes(grad_packed, at.time_project[...])
    at.wide[...] = at.grad_result[...] + modulate_back(
        grad_modulated, at.time_normed[...], time_inverse, row(4)
    )
    to_blocks(at.wide, at.grad_out)
    trade_start(at.grad_out, at.grad_in, at.grad_sent, at.grad_come)
    advance(reduction, 2)
    trade_wait(at.grad_out, at.grad_in, at.grad_sent, at.grad_come)
    from_blocks(at.grad_in, at.wide)

    scaled = (row(2) * at.wide[...]).astype(jnp.bfloat16)
    at.near_attended[...] = dot_lanes(scaled, at.space_merge[...]).astype(jnp.bfloat16)
    number = pair.send(at.near_attended, at.far_attended, partner)
    at.grad_keys[...] = jnp.zeros_like(at.grad_keys)
    at.grad_values[...] = jnp.zeros_like(at.grad_values)
    at.grad_queries[...] = jnp.zeros_like(at.grad_queries)
    for rows, grad_attended in (
        (slice(0, TOKENS), at.near_attended),
        (slice(TOKENS, 2 * TOKENS), at.far_attended),
    ):
        if rows.start:
            advance(reduction, 1)
            pair.arrived(number, at.far_attended, partner)
        for head, window, own in head_windows():
            probs = at.space_probs[head, rows, :]
            grads = score_grads(grad_attended, own, window, at.space_values, probs)
            at.grad_values[:, window] += dot_rows(
                probs[:, :TOKENS].astype(jnp.bfloat16), grad_attended[:, window] * own
            )
            at.grad_keys[:, window] += dot_rows(
                grads[:, :TOKENS], at.space_queries[rows, window] * own
            )
            if not rows.start:
                at.grad_queries[:, window] += dot(grads, at.space_keys[:, window] * own)
    grad_packed = join_packed(
        at.grad_packed, at.grad_queries[...], at.grad_keys[...], at.grad_values[...]
    )
    advance(reduction, 1)
    grad_modulated = dot_lanes(grad_packed, at.space_project[...])
    token_grads[...] = (
        at.wide[...]
        + modulate_back(grad_modulated, at.space_normed[...], at.space_inverse[...], row(1))
    ).astype(jnp.bfloat16)
    advance(reduction)
    unpack_final(at.final, merge_grads)
    for link in links + [pair, reducing]:
        link.finish()


def body(
    tokens, modulation, spatial_project, spatial_merge, temporal_project, temporal_merge, cotangent
):
    vmem = pl.BlockSpec(memory_space=pltpu.VMEM)
    blocks = (MEMBERS, 4, MODEL)
    result, token_grads, merge_grads = pl.pallas_call(
        clip_kernel,
        out_shape=[
            jax.ShapeDtypeStruct(blocks, jnp.bfloat16),
            jax.ShapeDtypeStruct((TOKENS, MODEL), jnp.bfloat16),
            jax.ShapeDtypeStruct((18, MODEL), jnp.float32),
        ],
        in_specs=[vmem] * 7,
        out_specs=[vmem] * 3,
        scratch_shapes=list(scratch_table().values()),
        compiler_params=pltpu.CompilerParams(
            collective_id=0, has_side_effects=True, vmem_limit_bytes=60 * 1024 * 1024
        ),
        cost_estimate=pl.CostEstimate(
            flops=3_000_000_000, bytes_accessed=4_000_000, transcendentals=500_000
        ),
        name="clip_step",
    )(
        tokens.reshape(TOKENS, MODEL),
        modulation,
        spatial_project,
        spatial_merge,
        temporal_project,
        temporal_merge,
        cotangent.reshape(blocks),
    )
    return (
        result.reshape(1, 16, 2, 4, MODEL),
        token_grads.reshape(1, 1, TOKENS, MODEL),
        merge_grads,
    )


def solution(mesh):
    in_specs = (
        P("dp", "seq", None, None),
        P("dp", None, None),
        P("seq", None),
        P("seq", None),
        P("seq", None),
        P("seq", None),
        P("dp", None, None, "seq", None),
    )
    out_specs = (P("dp", None, None, "seq", None), P("dp", "seq", None, None), P("seq", None))
    return jax.shard_map(body, mesh=mesh, in_specs=in_specs, out_specs=out_specs, check_vma=False)
```
